256 devices in a mesh: gx: 16 (over z, y_lo), gy: 8 (over x, core), gz: 2 (over y_hi).
Axes of the slice: x: 4, y: 4 (y_hi: 2, y_lo: 2; y = y_hi * 2 + y_lo), z: 8, core: 2. Of those that a mesh axis runs over, the one named last changes fastest.
Arguments:
- state: float32 [128, 4, 256, 1024], P('gz', None, 'gx', 'gy'), may hold values from -6 to 6
- metric: float32 [256, 1024], P('gx', 'gy'), may hold values from 0.25 to 1.75
- couple: float32 [128, 4, 256, 1024], P('gz', None, 'gx', 'gy'), may hold values from 1 to 4000
- base: float32 [128, 4, 256, 1024], P('gz', None, 'gx', 'gy'), may hold values from 0.5 to 2
Outputs:
- new_state: float32 [128, 4, 256, 1024], P('gz', None, 'gx', 'gy')
The draws below stay inside these ranges and needn't reach their ends.
All inputs are finite; a program needn't handle non-finite values.
Results may differ from the reference program's by a relative error of at most 0.0003.
Values sent between devices are 32-bit elements; how exact they have to be, the bound alone decides.
No kernel may reach another device: no remote copies, remote signals or barrier semaphores. Data moves between devices by JAX's collectives and lax.ppermute only.
A program may use at most 128 MiB of HBM per device.

```python
import math
import jax
import jax.numpy as jnp
from jax import lax

LEV = 128
FIELDS = 4
NX = 256
NY = 1024


def steps_of(rng, dims, cuts, low, high):
    gain, own = 1.0, jax.random.fold_in(rng, 6)
    for axis_at, parts in cuts:
        heights = jnp.exp(jax.random.uniform(jax.random.fold_in(own, axis_at), (parts,), jnp.float32, low / len(cuts), high / len(cuts)))
        gain = gain * jnp.repeat(heights, dims[axis_at] // parts).reshape([-1 if axis == axis_at else 1 for axis in range(len(dims))])
    return gain


def scatter_about(rng, dims, spread, most, split=(), held_as=jnp.bfloat16):
    level = steps_of(rng, dims, split, -0.22, 0.18) if split else 1.0
    drawn = jax.random.normal(rng, dims, jnp.float32) * spread * level
    return jnp.minimum(jnp.maximum(drawn, -most), most).astype(held_as)


def setup_inputs(seed: int = 0) -> dict:
    seeds = jax.random.split(jax.random.key(seed), 5)
    return {
        "state": scatter_about(seeds[0], (LEV, FIELDS, NX, NY), 1.0, 6.0, ((0, 2), (2, 16), (3, 8)), jnp.float32),
        "metric": jnp.clip(1.0 + 0.15 * jax.random.normal(seeds[1], (NX, NY), jnp.float32), 0.25, 1.75),
        "couple": jnp.clip(jnp.exp(math.log(4000.0) - 8.2940496 * jax.random.uniform(seeds[2], (LEV, FIELDS, NX, NY), jnp.float32) ** steps_of(seeds[2], (LEV, FIELDS, NX, NY), ((0, 2), (2, 16), (3, 8)), -0.2, 0.2)), 1.0, 4000.0),
        "base": jnp.clip(jnp.exp(math.log(2.0) - 1.3862944 * jax.random.uniform(seeds[3], (LEV, FIELDS, NX, NY), jnp.float32) ** steps_of(seeds[3], (LEV, FIELDS, NX, NY), ((0, 2), (2, 16), (3, 8)), -0.2, 0.2)), 0.5, 2.0),
    }


step_dt = 0.5
sound_sq = 1.0
hyper_nu = 0.01


def laplace(padded):
    return padded[:, 2:, 1:-1] + padded[:, :-2, 1:-1] + padded[:, 1:-1, 2:] + padded[:, 1:-1, :-2] - 4.0 * padded[:, 1:-1, 1:-1]


def forward_pass(lower, middle, upper, values, start):
    def advance(carry, item):
        c_prev, d_prev = carry
        low, mid, high, value = item
        denom = mid - low * c_prev
        c_next = high / denom
        d_next = (value + low * d_prev) / denom
        return (c_next, d_next), (c_next, d_next)

    final, (c_all, d_all) = lax.scan(advance, start, (lower, middle, upper, values), unroll=True)
    return c_all, d_all


def backward_pass(c_all, d_all, start):
    def retreat(x_next, item):
        c_here, d_here = item
        x_here = d_here + c_here * x_next
        return x_here, x_here

    final, x_all = lax.scan(retreat, start, (c_all, d_all), reverse=True, unroll=True)
    return x_all


def solve_columns(item):
    fields, coupling, weight = item
    levels = fields.shape[0]
    level_ids = jnp.arange(levels, dtype=jnp.int32)
    upper = jnp.where((level_ids < levels - 1)[:, None, None], coupling, jnp.float32(0.0))
    lower = jnp.concatenate([jnp.zeros_like(upper[:1]), upper[:-1]], axis=0)
    middle = weight + lower + upper
    values = weight * fields
    zeros = jnp.zeros(fields.shape[1:], jnp.float32)
    c_all, d_all = forward_pass(lower, middle, upper, values, (zeros, zeros))
    return backward_pass(c_all, d_all, zeros)


def reference(state, metric, couple, base):
    wind_u = state[:, 0]
    wind_v = state[:, 1]
    wind_w = state[:, 2]
    pressure = state[:, 3]
    padded = jnp.pad(pressure, ((0, 0), (0, 0), (2, 2)))
    padded = jnp.concatenate([padded[:, -2:], padded, padded[:, :2]], axis=1)
    new_u = wind_u - step_dt * 0.5 * metric * (padded[:, 3:-1, 2:-2] - padded[:, 1:-3, 2:-2])
    new_v = wind_v - step_dt * 0.5 * metric * (padded[:, 2:-2, 3:-1] - padded[:, 2:-2, 1:-3])
    diff_u = jnp.roll(new_u, -1, axis=1) - jnp.roll(new_u, 1, axis=1)
    padded_v = jnp.pad(new_v, ((0, 0), (0, 0), (1, 1)))
    diff_v = padded_v[:, :, 2:] - padded_v[:, :, :-2]
    divergence = 0.5 * metric * metric * (diff_u + diff_v)
    second = laplace(laplace(padded))
    new_p = pressure - step_dt * sound_sq * divergence - hyper_nu * second
    fields = jnp.stack([new_u, new_v, wind_w, new_p], axis=1)
    solved = lax.map(solve_columns, (jnp.moveaxis(fields, 1, 0), jnp.moveaxis(couple, 1, 0), jnp.moveaxis(base, 1, 0)))
    return jnp.moveaxis(solved, 0, 1)
```

```python
import functools

import jax
import jax.numpy as jnp
from jax import lax
from jax.experimental import pallas as pl
from jax.experimental.pallas import tpu as pltpu
from jax.sharding import PartitionSpec as P

step_dt = 0.5
sound_sq = 1.0
hyper_nu = 0.01

f32 = jnp.float32
ANY = pl.BlockSpec(memory_space=pl.ANY)
VM = pl.BlockSpec(memory_space=pltpu.VMEM)
LIMIT = 32 * 1024 * 1024


def loop(count, body, carry, unroll):
    assert count % unroll == 0

    def several(i, carry):
        for j in range(unroll):
            carry = body(i * unroll + j, carry)
        return carry

    return lax.fori_loop(0, count // unroll, several, carry)


def row_ids(rows):
    return lax.broadcasted_iota(jnp.int32, (rows, 128), 0)


def lane_ids(rows):
    return lax.broadcasted_iota(jnp.int32, (rows, 128), 1)


def order(levels):
    top = lax.axis_index("gz")
    sign = 1 - 2 * top
    return top, sign, top * (levels - 1), top * (levels - 2)


def load_and_pack_x(state, metric, up, low_side, high_side, sems):
    levels = up.shape[0]
    copies = [
        pltpu.make_async_copy(state.at[:, field], up.at[:, slot], sems.at[slot])
        for slot, field in ((0, 0), (1, 3))
    ]
    for copy in copies:
        copy.start()
    for row, out in ((0, low_side), (15, high_side)):
        out[3 * levels : 3 * levels + 8, :] = jnp.broadcast_to(metric[row : row + 1, :], (8, 128))
    for copy in copies:
        copy.wait()
    flat = up.reshape(levels * 32, 128)
    for out, near, far in ((low_side, 0, 1), (high_side, 15, 14)):
        for part, row in enumerate((16 + near, 16 + far, near)):
            for base in range(0, levels, 8):
                out[part * levels + base : part * levels + base + 8, :] = flat[
                    pl.ds(base * 32 + row, 8, stride=32), :
                ]


def block_of(rows):
    return lax.rem(lane_ids(rows) + 2, 128) // 4


def factor(state, couple, base, metric, up, vw, part_a, part_b, part_c, edges, resist, pair, weights, sems):
    levels = vw.shape[0]
    top, sign, first, link = order(levels)
    chunk = levels // 4
    wind = [
        pltpu.make_async_copy(state.at[:, 1 + slot], vw.at[:, slot], sems.at[8 + slot]) for slot in range(2)
    ]
    copies = []
    for j in range(4):
        at = pl.ds(top * (levels - chunk) + sign * (j * chunk), chunk)
        copies.append(
            [
                pltpu.make_async_copy(couple.at[at], pair.at[at], sems.at[2 * j]),
                pltpu.make_async_copy(base.at[at], weights.at[at], sems.at[2 * j + 1]),
            ]
        )
    for group in copies:
        for copy in group:
            copy.start()
    for copy in wind:
        copy.start()

    def step(k, carry):
        g, before = carry
        here = first + sign * k
        weight = weights[here]
        after = pair[link + sign * k]
        total = weight + before * g
        inverse = 1.0 / (total + after)
        part_a[here] = weight * inverse
        part_b[here] = before * inverse
        part_c[here] = after * inverse
        return total * inverse, after

    zeros = jnp.zeros((4, 16, 128), f32)
    carry = (zeros, zeros)
    for j in range(4):
        if j == 0:
            for copy in copies[0] + copies[1]:
                copy.wait()
        elif j < 3:
            for copy in copies[j + 1]:
                copy.wait()
        count = chunk if j < 3 else chunk - 1
        start = j * chunk
        if count % 4 == 0:
            carry = loop(count, lambda k, c: step(start + k, c), carry, 4)
        else:
            carry = loop(count, lambda k, c: step(start + k, c), carry, 3)
    g, before = carry
    here = first + sign * (levels - 1)
    weight = weights[here]
    inverse = 1.0 / (weight + before * g)
    part_a[here] = weight * inverse
    part_b[here] = before * inverse
    part_c[here] = inverse
    outward = jnp.where(top == 0, 1.0 / pair[levels - 1], zeros)
    resist[...] = inverse + outward

    for copy in wind:
        copy.wait()
    block = block_of(16)
    for half in range(2):

        def gather(i, carry):
            kept_p, kept_v = carry
            level = half * (levels // 2) + i
            mine = block == i
            kept_p = jnp.where(mine, pltpu.roll(up[level, 1], 4 * i, 1), kept_p)
            kept_v = jnp.where(mine, pltpu.roll(vw[level, 0], 4 * i, 1), kept_v)
            return kept_p, kept_v

        kept = jnp.zeros((16, 128), f32)
        kept_p, kept_v = loop(levels // 2, gather, (kept, kept), 4)
        edges[16 * half : 16 * half + 16, :] = kept_p
        edges[32 + 16 * half : 48 + 16 * half, :] = kept_v
    own = jnp.where(block == 0, metric[...], 0.0)
    for shift in (4, 8, 16, 32, 64):
        own = own + pltpu.roll(own, shift, 1)
    edges[64:80, :] = own


def pack_y(edges, low_halo, high_halo, out):
    levels = (low_halo.shape[0] - 8) // 3
    out[0:80, :] = edges[...]
    block = block_of(8)
    row = row_ids(8)
    kept = jnp.zeros((8, 128), f32)
    for half in range(2):

        def gather(i, kept):
            level = half * (levels // 2) + i
            low = jnp.broadcast_to(low_halo[pl.ds(level, 1), :], (8, 128))
            high = jnp.broadcast_to(high_halo[pl.ds(level, 1), :], (8, 128))
            both = pltpu.roll(jnp.where(row == 2 * half, low, high), 4 * i, 1)
            return jnp.where((block == i) & (row // 2 == half), both, kept)

        kept = loop(levels // 2, gather, kept, 4)
    out[80:88, :] = kept


def interior(up, vw, low_halo, high_halo, metric, part_a, part_b, partial, done):
    levels = up.shape[0]
    top, sign, first, link = order(levels)
    row = row_ids(16)
    lane = lane_ids(16)
    m = metric[...]
    slope = step_dt * 0.5 * m
    spread = 0.5 * step_dt * sound_sq * m * m
    slope_low = step_dt * 0.5 * low_halo[3 * levels : 3 * levels + 1, :]
    slope_high = step_dt * 0.5 * high_halo[3 * levels : 3 * levels + 1, :]

    def east(z, far=1):
        return jnp.where(lane >= 128 - far, 0.0, pltpu.roll(z, 128 - far, 1))

    def west(z, far=1):
        return jnp.where(lane < far, 0.0, pltpu.roll(z, far, 1))

    def step(k, carry):
        d_u, d_w = carry
        l = first + sign * k
        p = up[l, 1]
        u = up[l, 0]
        v = vw[l, 0]
        w = vw[l, 1]
        near_low = low_halo[pl.ds(l, 1), :]
        far_low = low_halo[pl.ds(levels + l, 1), :]
        u_low = low_halo[pl.ds(2 * levels + l, 1), :]
        near_high = high_halo[pl.ds(l, 1), :]
        far_high = high_halo[pl.ds(levels + l, 1), :]
        u_high = high_halo[pl.ds(2 * levels + l, 1), :]
        before = jnp.where(row == 0, near_low, pltpu.roll(p, 1, 0))
        after = jnp.where(row == 15, near_high, pltpu.roll(p, 15, 0))
        before2 = jnp.where(row == 0, far_low, pltpu.roll(before, 1, 0))
        after2 = jnp.where(row == 15, far_high, pltpu.roll(after, 15, 0))
        u1 = u - slope * (after - before)
        v1 = v - slope * (east(p) - west(p))
        u1_low = u_low - slope_low * (p[0:1] - far_low)
        u1_high = u_high - slope_high * (far_high - p[15:16])
        diff_u = jnp.where(row == 15, u1_high, pltpu.roll(u1, 15, 0)) - jnp.where(
            row == 0, u1_low, pltpu.roll(u1, 1, 0)
        )
        diff_v = east(v1) - west(v1)
        sides = before + after
        cross = 2.0 * sides - 8.0 * p
        second = (before2 + after2) + (east(p, 2) + west(p, 2)) + (east(cross) + west(cross)) - 8.0 * sides + 20.0 * p
        p1 = p - spread * (diff_u + diff_v) - hyper_nu * second
        partial[l, 0] = v1
        partial[l, 1] = p1
        d_u = part_a[l, 0] * u1 + part_b[l, 0] * d_u
        d_w = part_a[l, 2] * w + part_b[l, 2] * d_w
        done[l, 0] = d_u
        done[l, 1] = d_w
        return d_u, d_w

    zeros = jnp.zeros((16, 128), f32)
    loop(levels, step, (zeros, zeros), 4)


def finish_forward(partial, done, part_a, part_b, metric, edges, left, right, resist, solved, out, fix_v, fix_p):
    levels = partial.shape[0]
    top, sign, first, link = order(levels)
    lane = lane_ids(16)
    row = row_ids(16)
    place = lax.rem(lane + 2, 4)
    m = edges[64:80, :]
    slope = step_dt * 0.5 * m
    spread = 0.5 * step_dt * sound_sq * m * m
    slope_left = step_dt * 0.5 * left[64:80, :]
    slope_right = step_dt * 0.5 * right[64:80, :]

    def shift(z, by):
        return pltpu.roll(z, by % 128, 1)

    for half in range(2):
        at = 16 * half

        def cross(side):
            p = side[at : at + 16, :]
            low = side[80 + 2 * half : 81 + 2 * half, :]
            high = side[81 + 2 * half : 82 + 2 * half, :]
            before = jnp.where(row == 0, low, pltpu.roll(p, 1, 0))
            after = jnp.where(row == 15, high, pltpu.roll(p, 15, 0))
            return 2.0 * (before + after) - 8.0 * p

        p_own = edges[at : at + 16, :]
        p_left = left[at : at + 16, :]
        p_right = right[at : at + 16, :]
        v_left = left[32 + at : 48 + at, :]
        v_right = right[32 + at : 48 + at, :]
        second = (
            jnp.where(place >= 2, shift(p_left, 2), shift(p_right, -2))
            + jnp.where(place == 2, shift(cross(left), 1), 0.0)
            + jnp.where(place == 1, shift(cross(right), -1), 0.0)
        )
        own_v = jnp.where(
            place == 2, slope * shift(p_left, 1), jnp.where(place == 1, -slope * shift(p_right, -1), 0.0)
        )
        v1_left = v_left - slope_left * (shift(p_own, -1) - shift(p_left, 1))
        v1_right = v_right - slope_right * (shift(p_right, -1) - shift(p_own, 1))
        diff_v = jnp.where(
            place == 2,
            -shift(v1_left, 1),
            jnp.where(place == 3, -shift(own_v, 1), jnp.where(place == 1, shift(v1_right, -1), shift(own_v, -1))),
        )
        fix_v[half] = own_v
        fix_p[half] = -spread * diff_v - hyper_nu * second

    edge = (lane >= 126) | (lane < 2)

    def step(k, carry):
        d_v, d_p = carry
        l = first + sign * k
        half = l // (levels // 2)
        back = lax.rem(128 - 4 * lax.rem(l, levels // 2), 128)
        v1 = partial[l, 0] + jnp.where(edge, pltpu.roll(fix_v[half], back, 1), 0.0)
        p1 = partial[l, 1] + jnp.where(edge, pltpu.roll(fix_p[half], back, 1), 0.0)
        d_v = part_a[l, 1] * v1 + part_b[l, 1] * d_v
        d_p = part_a[l, 3] * p1 + part_b[l, 3] * d_p
        solved[l, 0] = d_v
        solved[l, 1] = d_p
        return d_v, d_p

    zeros = jnp.zeros((16, 128), f32)
    d_v, d_p = loop(levels, step, (zeros, zeros), 4)
    last = first + sign * (levels - 1)
    out[0, 0] = done[last, 0]
    out[0, 1] = d_v
    out[0, 2] = done[last, 1]
    out[0, 3] = d_p
    out[1] = resist[...]


def back_substitute(done, solved, part_c, mine, other, out, x_ref, sems):
    levels = done.shape[0]
    top, sign, first, link = order(levels)
    last = first + sign * (levels - 1)
    x = mine[0] + (other[0] - mine[0]) * (part_c[last] / (mine[1] + other[1]))
    x_ref[last] = x
    chunk = levels // 4
    copies = []

    def step(k, x):
        l = last - sign * k
        c = part_c[l]
        parts = []
        for field in range(4):
            d = (done, solved)[field % 2][l, field // 2]
            parts.append(d + c[field] * x[field])
        x = jnp.stack(parts)
        x_ref[l] = x
        return x

    for j in range(4):
        start = j * chunk + (j == 0)
        count = chunk - (j == 0)
        x = loop(count, lambda k, x: step(start + k, x), x, 4 if count % 4 == 0 else 3)
        at = pl.ds((1 - top) * (levels - chunk) - sign * (j * chunk), chunk)
        copy = pltpu.make_async_copy(x_ref.at[at], out.at[at], sems.at[j])
        copy.start()
        copies.append(copy)
    for copy in copies:
        copy.wait()


def near(shape):
    return pltpu.VMEM(shape, f32)


def plain(shape):
    return jax.ShapeDtypeStruct(shape, f32)


def call(body, ins, outs, scratch, cost=0, name=None):
    def run(*args):
        return pl.pallas_call(
            body,
            in_specs=ins,
            out_specs=[s for s, _ in outs],
            out_shape=[o for _, o in outs],
            scratch_shapes=scratch,
            name=name,
            cost_estimate=pl.CostEstimate(flops=cost, bytes_accessed=cost, transcendentals=0) if cost else None,
            compiler_params=pltpu.CompilerParams(vmem_limit_bytes=LIMIT),
        )(*args)

    return run


def shards(state, metric, couple, base):
    levels = state.shape[0]
    nx, ny = lax.axis_size("gx"), lax.axis_size("gy")
    dma = pltpu.SemaphoreType.DMA
    edge_rows = 3 * levels + 8
    full = (levels, 4, 16, 128)
    two = (levels, 2, 16, 128)

    up, low_side, high_side = call(
        load_and_pack_x,
        [ANY, VM],
        [(VM, near(two)), (VM, plain((edge_rows, 128))), (VM, plain((edge_rows, 128)))],
        [dma((2,))],
        name="load_and_pack_x",
    )(state, metric)
    low_halo = lax.ppermute(high_side, "gx", [(i, (i + 1) % nx) for i in range(nx)])
    high_halo = lax.ppermute(low_side, "gx", [((i + 1) % nx, i) for i in range(nx)])

    vw, part_a, part_b, part_c, edges, resist = call(
        factor,
        [ANY, ANY, ANY, VM, VM],
        [
            (VM, near(two)),
            (VM, near(full)),
            (VM, near(full)),
            (VM, near(full)),
            (VM, near((80, 128))),
            (VM, near((4, 16, 128))),
        ],
        [pltpu.VMEM(full, f32), pltpu.VMEM(full, f32), dma((10,))],
        cost=8 * 1024 * 1024,
        name="factor",
    )(state, couple, base, metric, up)

    packed = call(
        pack_y, [VM, VM, VM], [(VM, plain((88, 128)))], [], name="pack_y"
    )(edges, low_halo, high_halo)[0]
    left = lax.ppermute(packed, "gy", [(i, i + 1) for i in range(ny - 1)])
    right = lax.ppermute(packed, "gy", [(i + 1, i) for i in range(ny - 1)])

    partial, done = call(
        interior,
        [VM] * 7,
        [(VM, near(two)), (VM, near(two))],
        [],
        cost=8 * 1024 * 1024,
        name="interior",
    )(up, vw, low_halo, high_halo, metric, part_a, part_b)

    solved, mine = call(
        finish_forward,
        [VM] * 9,
        [(VM, near(two)), (VM, plain((2, 4, 16, 128)))],
        [pltpu.VMEM((2, 16, 128), f32), pltpu.VMEM((2, 16, 128), f32)],
        name="finish_forward",
    )(partial, done, part_a, part_b, metric, packed, left, right, resist)
    other = lax.ppermute(mine, "gz", [(0, 1), (1, 0)])

    return call(
        back_substitute,
        [VM] * 5,
        [(ANY, plain(full))],
        [pltpu.VMEM(full, f32), dma((4,))],
        name="back_substitute",
    )(done, solved, part_c, mine, other)[0]


def solution(mesh):
    in_specs = (
        P("gz", None, "gx", "gy"),
        P("gx", "gy"),
        P("gz", None, "gx", "gy"),
        P("gz", None, "gx", "gy"),
    )
    out_specs = P("gz", None, "gx", "gy")
    return jax.shard_map(shards, mesh=mesh, in_specs=in_specs, out_specs=out_specs, check_vma=False)
```

```python
import functools

import jax
import jax.numpy as jnp
from jax import lax
from jax.experimental import pallas as pl
from jax.experimental.pallas import tpu as pltpu
from jax.sharding import PartitionSpec as P

step_dt = 0.5
sound_sq = 1.0
hyper_nu = 0.01

f32 = jnp.float32
HB = pl.BlockSpec(memory_space=pltpu.HBM)
VM = pl.BlockSpec(memory_space=pltpu.VMEM)
LIMIT = 32 * 1024 * 1024


def loop(count, body, carry, unroll):
    assert count % unroll == 0

    def several(i, carry):
        for j in range(unroll):
            carry = body(i * unroll + j, carry)
        return carry

    return lax.fori_loop(0, count // unroll, several, carry)


def row_ids(rows):
    return lax.broadcasted_iota(jnp.int32, (rows, 128), 0)


def lane_ids(rows):
    return lax.broadcasted_iota(jnp.int32, (rows, 128), 1)


def order(levels):
    top = lax.axis_index("gz")
    sign = 1 - 2 * top
    return top, sign, top * (levels - 1), top * (levels - 2)


def pack_x(state, metric, low_side, high_side, sems):
    levels = state.shape[0]
    copies = []
    for out, rows in ((low_side, (0, 1, 0)), (high_side, (15, 14, 15))):
        for part, (field, row) in enumerate(zip((3, 3, 0), rows)):
            copies.append((state.at[:, field, row], out.at[pl.ds(part * levels, levels)]))
        copies.append((metric.at[pl.ds(rows[0], 1)], out.at[pl.ds(3 * levels, 1)]))
    copies = [pltpu.make_async_copy(src, dst, sems.at[i]) for i, (src, dst) in enumerate(copies)]
    for copy in copies:
        copy.start()
    for copy in copies:
        copy.wait()


def block_of(rows):
    return lax.rem(lane_ids(rows) + 2, 128) // 4


def factor(state, couple, base, metric, fields, own_metric, part_a, part_b, part_c, edges, resist, pair, weights, sems):
    levels = fields.shape[0]
    top, sign, first, link = order(levels)
    chunk = levels // 4
    early = [
        pltpu.make_async_copy(state.at[:, field], fields.at[:, field], sems.at[8 + i]) for i, field in enumerate((3, 1))
    ]
    early.append(pltpu.make_async_copy(metric, own_metric, sems.at[10]))
    late = [
        pltpu.make_async_copy(state.at[:, field], fields.at[:, field], sems.at[11 + i]) for i, field in enumerate((0, 2))
    ]
    copies = []
    for j in range(4):
        at = pl.ds(top * (levels - chunk) + sign * (j * chunk), chunk)
        copies.append(
            [
                pltpu.make_async_copy(couple.at[at], pair.at[at], sems.at[2 * j]),
                pltpu.make_async_copy(base.at[at], weights.at[at], sems.at[2 * j + 1]),
            ]
        )
    for copy in early + [copy for group in copies for copy in group] + late:
        copy.start()

    for copy in early:
        copy.wait()
    block = block_of(16)
    for half in range(2):

        def gather(i, carry):
            kept_p, kept_v = carry
            moved = []
            for j in range(16):
                at = 16 * i + j
                level = half * (levels // 2) + at
                moved.append(
                    (block == at, pltpu.roll(fields[level, 3], 4 * at, 1), pltpu.roll(fields[level, 1], 4 * at, 1))
                )
            for mine, p, v in moved:
                kept_p = jnp.where(mine, p, kept_p)
                kept_v = jnp.where(mine, v, kept_v)
            return kept_p, kept_v

        kept = jnp.zeros((16, 128), f32)
        kept_p, kept_v = lax.fori_loop(0, levels // 32, gather, (kept, kept))
        edges[16 * half : 16 * half + 16, :] = kept_p
        edges[32 + 16 * half : 48 + 16 * half, :] = kept_v
    own = jnp.where(block == 0, own_metric[...], 0.0)
    for shift in (4, 8, 16, 32, 64):
        own = own + pltpu.roll(own, shift, 1)
    edges[64:80, :] = own

    def step(k, carry):
        g, before = carry
        here = first + sign * k
        weight = weights[here]
        after = pair[link + sign * k]
        total = weight + before * g
        inverse = 1.0 / (total + after)
        part_a[here] = weight * inverse
        part_b[here] = before * inverse
        part_c[here] = after * inverse
        return total * inverse, after

    zeros = jnp.zeros((4, 16, 128), f32)
    carry = (zeros, zeros)
    for j in range(4):
        if j == 0:
            for copy in copies[0] + copies[1]:
                copy.wait()
        elif j < 3:
            for copy in copies[j + 1]:
                copy.wait()
        count = chunk if j < 3 else chunk - 1
        start = j * chunk
        if count % 8 == 0:
            carry = loop(count, lambda k, c: step(start + k, c), carry, 8)
        else:
            carry = loop(count, lambda k, c: step(start + k, c), carry, 5)
    g, before = carry
    here = first + sign * (levels - 1)
    weight = weights[here]
    inverse = 1.0 / (weight + before * g)
    part_a[here] = weight * inverse
    part_b[here] = before * inverse
    part_c[here] = inverse
    outward = jnp.where(top == 0, 1.0 / pair[levels - 1], zeros)
    resist[...] = inverse + outward
    for copy in late:
        copy.wait()


def pack_y(edges, low_halo, high_halo, out):
    levels = (low_halo.shape[0] - 8) // 3
    block = block_of(8)
    row = row_ids(8)
    kept = jnp.zeros((8, 128), f32)
    for half in range(2):

        def gather(i, kept):
            moved = []
            for j in range(32):
                at = 32 * i + j
                level = half * (levels // 2) + at
                low = jnp.broadcast_to(low_halo[pl.ds(level, 1), :], (8, 128))
                high = jnp.broadcast_to(high_halo[pl.ds(level, 1), :], (8, 128))
                both = pltpu.roll(jnp.where(row == 2 * half, low, high), 4 * at, 1)
                moved.append(((block == at) & (row // 2 == half), both))
            for mine, both in moved:
                kept = jnp.where(mine, both, kept)
            return kept

        kept = lax.fori_loop(0, levels // 64, gather, kept)
    out[0:80, :] = edges[...]
    out[80:88, :] = kept


def interior(fields, low_halo, high_halo, metric, part_a, part_b, partial, done):
    levels = fields.shape[0]
    top, sign, first, link = order(levels)
    row = row_ids(16)
    m = metric[...]
    slope = step_dt * 0.5 * m
    spread = 0.5 * step_dt * sound_sq * m * m
    slope_low = step_dt * 0.5 * low_halo[3 * levels : 3 * levels + 1, :]
    slope_high = step_dt * 0.5 * high_halo[3 * levels : 3 * levels + 1, :]
    batch = 8

    def east(z):
        return pltpu.roll(z, 127, 1)

    def west(z):
        return pltpu.roll(z, 1, 1)

    def below(z, edge):
        return jnp.where(row == 0, edge, pltpu.roll(z, 1, 0))

    def above(z, edge):
        return jnp.where(row == 15, edge, pltpu.roll(z, 15, 0))

    def several(i, carry):
        d_u, d_w = carry
        ls = [first + sign * (i * batch + j) for j in range(batch)]
        pieces = []
        for l in ls:
            p = fields[l, 3]
            u = fields[l, 0]
            v = fields[l, 1]
            near_low = low_halo[pl.ds(l, 1), :]
            far_low = low_halo[pl.ds(levels + l, 1), :]
            u_low = low_halo[pl.ds(2 * levels + l, 1), :]
            near_high = high_halo[pl.ds(l, 1), :]
            far_high = high_halo[pl.ds(levels + l, 1), :]
            u_high = high_halo[pl.ds(2 * levels + l, 1), :]
            drive = fields[l, 2] * part_a[l, 2]
            pieces.append(
                (p, u, v, near_low, far_low, u_low, near_high, far_high, u_high, part_a[l, 0], part_b[l, 0], drive, part_b[l, 2])
            )
        results = []
        for p, u, v, near_low, far_low, u_low, near_high, far_high, u_high, a_u, b_u, drive, b_w in pieces:
            before = below(p, near_low)
            after = above(p, near_high)
            sides = before + after
            outer = below(before, far_low) + above(after, far_high)
            p_east, p_west = east(p), west(p)
            u1 = u - slope * (after - before)
            v1 = v - slope * (p_east - p_west)
            u1_low = u_low - slope_low * (p[0:1] - far_low)
            u1_high = u_high - slope_high * (far_high - p[15:16])
            diff_u = above(u1, u1_high) - below(u1, u1_low)
            diff_v = east(v1) - west(v1)
            inner = (p_east + p_west) + 2.0 * sides - 8.0 * p
            second = outer + (east(inner) + west(inner)) - 8.0 * sides + 18.0 * p
            p1 = p - spread * (diff_u + diff_v) - hyper_nu * second
            results.append((v1, p1, a_u * u1, b_u, drive, b_w))
        for l, (v1, p1, drive_u, b_u, drive_w, b_w) in zip(ls, results):
            partial[l, 0] = v1
            partial[l, 1] = p1
            d_u = drive_u + b_u * d_u
            d_w = drive_w + b_w * d_w
            done[l, 0] = d_u
            done[l, 1] = d_w
        return d_u, d_w

    zeros = jnp.zeros((16, 128), f32)
    lax.fori_loop(0, levels // batch, several, (zeros, zeros))


def finish_forward(partial, done, part_a, part_b, edges, left, right, resist, solved, out, fix_v, fix_p):
    turn = lax.axis_index("gy")
    left = jnp.where(turn == 0, 0.0, left[...])
    right = jnp.where(turn == lax.axis_size("gy") - 1, 0.0, right[...])
    edges = edges[...]
    levels = partial.shape[0]
    top, sign, first, link = order(levels)
    lane = lane_ids(16)
    row = row_ids(16)
    place = lax.rem(lane + 2, 4)
    m = edges[64:80, :]
    slope = step_dt * 0.5 * m
    spread = 0.5 * step_dt * sound_sq * m * m
    slope_left = step_dt * 0.5 * left[64:80, :]
    slope_right = step_dt * 0.5 * right[64:80, :]

    def shift(z, by):
        return pltpu.roll(z, by % 128, 1)

    for half in range(2):
        at = 16 * half

        def sides_of(side):
            p = side[at : at + 16, :] - edges[at : at + 16, :]
            ends = 80 + 2 * half
            low = side[ends : ends + 1, :] - edges[ends : ends + 1, :]
            high = side[ends + 1 : ends + 2, :] - edges[ends + 1 : ends + 2, :]
            before = jnp.where(row == 0, low, pltpu.roll(p, 1, 0))
            after = jnp.where(row == 15, high, pltpu.roll(p, 15, 0))
            return p, 2.0 * (before + after) - 8.0 * p

        p_own = edges[at : at + 16, :]
        p_left, cross_left = sides_of(left)
        p_right, cross_right = sides_of(right)
        p_east, p_west = shift(p_own, -1), shift(p_own, 1)
        v1_own = edges[32 + at : 48 + at, :] - slope * (p_east - p_west)
        v1_left = left[32 + at : 48 + at, :] - slope_left * (p_east - shift(left[at : at + 16, :], 1))
        v1_right = right[32 + at : 48 + at, :] - slope_right * (shift(right[at : at + 16, :], -1) - p_west)
        second = (
            jnp.where(place >= 2, shift(p_left, 2), shift(p_right, -2))
            + jnp.where(place == 2, shift(cross_left, 1), 0.0)
            + jnp.where(place == 1, shift(cross_right, -1), 0.0)
        )
        own_v = jnp.where(
            place == 2, slope * shift(p_left, 1), jnp.where(place == 1, -slope * shift(p_right, -1), 0.0)
        )
        diff_v = jnp.where(
            place == 2,
            shift(v1_own - v1_left, 1),
            jnp.where(
                place == 3,
                -shift(own_v, 1),
                jnp.where(place == 1, shift(v1_right - v1_own, -1), shift(own_v, -1)),
            ),
        )
        fix_v[half] = own_v
        fix_p[half] = -spread * diff_v - hyper_nu * second

    edge = (lane >= 126) | (lane < 2)
    batch = 16

    def segment(turn, carry):
        half = top + sign * turn
        all_v = fix_v[half]
        all_p = fix_p[half]

        def several(i, carry):
            d_v, d_p = carry
            ls = [first + sign * (turn * (levels // 2) + i * batch + j) for j in range(batch)]
            drives = []
            for l in ls:
                back = lax.rem(128 - 4 * (l - half * (levels // 2)), 128)
                v1 = partial[l, 0] + jnp.where(edge, pltpu.roll(all_v, back, 1), 0.0)
                p1 = partial[l, 1] + jnp.where(edge, pltpu.roll(all_p, back, 1), 0.0)
                drives.append((part_a[l, 1] * v1, part_b[l, 1], part_a[l, 3] * p1, part_b[l, 3]))
            for l, (drive_v, b_v, drive_p, b_p) in zip(ls, drives):
                d_v = drive_v + b_v * d_v
                d_p = drive_p + b_p * d_p
                solved[l, 0] = d_v
                solved[l, 1] = d_p
            return d_v, d_p

        return lax.fori_loop(0, levels // (2 * batch), several, carry)

    zeros = jnp.zeros((16, 128), f32)
    d_v, d_p = segment(1, segment(0, (zeros, zeros)))
    last = first + sign * (levels - 1)
    out[0, 0] = done[last, 0]
    out[0, 1] = d_v
    out[0, 2] = done[last, 1]
    out[0, 3] = d_p
    out[1] = resist[...]


def back_substitute(done, solved, part_c, mine, other, out, x_ref, sems):
    levels = done.shape[0]
    top, sign, first, link = order(levels)
    last = first + sign * (levels - 1)
    x = mine[0] + (other[0] - mine[0]) * (part_c[last] / (mine[1] + other[1]))
    x_ref[last] = x
    chunk = levels // 8
    copies = []

    def several(ks, x):
        ls = [last - sign * k for k in ks]
        loaded = [
            (part_c[l], [done[l, 0], solved[l, 0], done[l, 1], solved[l, 1]]) for l in ls
        ]
        for l, (c, d) in zip(ls, loaded):
            x = jnp.stack(d) + c * x
            x_ref[l] = x
        return x

    for j in range(8):
        ks = list(range(j * chunk + (j == 0), (j + 1) * chunk))
        for i in range(0, len(ks), 2):
            x = several(ks[i : i + 2], x)
        at = pl.ds((1 - top) * (levels - chunk) - sign * (j * chunk), chunk)
        copy = pltpu.make_async_copy(x_ref.at[at], out.at[at], sems.at[j])
        copy.start()
        copies.append(copy)
    for copy in copies:
        copy.wait()


def near(shape):
    return pltpu.VMEM(shape, f32)


def plain(shape):
    return jax.ShapeDtypeStruct(shape, f32)


def call(body, ins, outs, scratch=(), cost=0, name=None, aliases=None):
    def run(*args):
        return pl.pallas_call(
            body,
            in_specs=ins,
            out_specs=[VM] * len(outs),
            out_shape=outs,
            scratch_shapes=list(scratch),
            name=name,
            input_output_aliases=aliases or {},
            cost_estimate=pl.CostEstimate(flops=cost, bytes_accessed=cost, transcendentals=0) if cost else None,
            compiler_params=pltpu.CompilerParams(vmem_limit_bytes=LIMIT),
        )(*args)

    return run


def far(x):
    return pltpu.with_memory_space_constraint(x, pltpu.HBM)


def shards(state, metric, couple, base):
    levels = state.shape[0]
    nx, ny = lax.axis_size("gx"), lax.axis_size("gy")
    dma = pltpu.SemaphoreType.DMA
    side = (3 * levels + 8, 128)
    full = (levels, 4, 16, 128)
    two = (levels, 2, 16, 128)
    state, metric, couple, base = far(state), far(metric), far(couple), far(base)

    low_side, high_side = call(
        pack_x, [HB, HB], [plain(side), plain(side)], [dma((8,))], name="pack_x"
    )(state, metric)
    low_halo = lax.ppermute(high_side, "gx", [(i, (i + 1) % nx) for i in range(nx)])
    high_halo = lax.ppermute(low_side, "gx", [((i + 1) % nx, i) for i in range(nx)])

    fields, own_metric, part_a, part_b, part_c, edges, resist = call(
        factor,
        [HB, HB, HB, HB],
        [near(full), near((16, 128)), near(full), near(full), near(full), near((80, 128)), near((4, 16, 128))],
        [pltpu.VMEM(full, f32), pltpu.VMEM(full, f32), dma((13,))],
        cost=8 * 1024 * 1024,
        name="factor",
    )(state, couple, base, metric)

    packed = call(pack_y, [VM] * 3, [plain((88, 128))], name="pack_y")(edges, low_halo, high_halo)[0]
    left = lax.ppermute(packed, "gy", [(i, (i + 1) % ny) for i in range(ny)])
    right = lax.ppermute(packed, "gy", [((i + 1) % ny, i) for i in range(ny)])

    partial, done = call(
        interior,
        [VM] * 6,
        [near(two), near(two)],
        cost=8 * 1024 * 1024,
        name="interior",
    )(fields, low_halo, high_halo, own_metric, part_a, part_b)

    solved, mine = call(
        finish_forward,
        [VM] * 8,
        [near(two), plain((2, 4, 16, 128))],
        [pltpu.VMEM((2, 16, 128), f32), pltpu.VMEM((2, 16, 128), f32)],
        name="finish_forward",
    )(partial, done, part_a, part_b, packed, left, right, resist)
    other = lax.ppermute(mine, "gz", [(0, 1), (1, 0)])

    return pl.pallas_call(
        back_substitute,
        in_specs=[VM] * 5,
        out_specs=pl.BlockSpec(memory_space=pl.ANY),
        out_shape=plain(full),
        scratch_shapes=[pltpu.VMEM(full, f32), dma((8,))],
        name="back_substitute",
        compiler_params=pltpu.CompilerParams(vmem_limit_bytes=LIMIT),
    )(done, solved, part_c, mine, other)


def solution(mesh):
    in_specs = (
        P("gz", None, "gx", "gy"),
        P("gx", "gy"),
        P("gz", None, "gx", "gy"),
        P("gz", None, "gx", "gy"),
    )
    out_specs = P("gz", None, "gx", "gy")
    return jax.shard_map(shards, mesh=mesh, in_specs=in_specs, out_specs=out_specs, check_vma=False)
```

```python
import functools

import jax
import jax.numpy as jnp
from jax import lax
from jax.experimental import pallas as pl
from jax.experimental.pallas import tpu as pltpu
from jax.sharding import PartitionSpec as P

step_dt = 0.5
sound_sq = 1.0
hyper_nu = 0.01

f32 = jnp.float32
HB = pl.BlockSpec(memory_space=pltpu.HBM)
VM = pl.BlockSpec(memory_space=pltpu.VMEM)
LIMIT = 32 * 1024 * 1024


def loop(count, body, carry, unroll):
    assert count % unroll == 0

    def several(i, carry):
        for j in range(unroll):
            carry = body(i * unroll + j, carry)
        return carry

    return lax.fori_loop(0, count // unroll, several, carry)


def row_ids(rows):
    return lax.broadcasted_iota(jnp.int32, (rows, 128), 0)


def lane_ids(rows):
    return lax.broadcasted_iota(jnp.int32, (rows, 128), 1)


def order(levels):
    top = lax.axis_index("gz")
    sign = 1 - 2 * top
    return top, sign, top * (levels - 1), top * (levels - 2)


def pack_x(state, metric, low_side, high_side, sems):
    levels = state.shape[0]
    copies = []
    for out, rows in ((low_side, (0, 1, 0)), (high_side, (15, 14, 15))):
        for part, (field, row) in enumerate(zip((3, 3, 0), rows)):
            copies.append((state.at[:, field, row], out.at[pl.ds(part * levels, levels)]))
        copies.append((metric.at[pl.ds(rows[0], 1)], out.at[pl.ds(3 * levels, 1)]))
    copies = [pltpu.make_async_copy(src, dst, sems.at[i]) for i, (src, dst) in enumerate(copies)]
    for copy in copies:
        copy.start()
    for copy in copies:
        copy.wait()


def block_of(rows):
    return lax.rem(lane_ids(rows) + 2, 128) // 4


def factor(state, couple, base, metric, fields, own_metric, part_a, part_b, part_c, edges, sides, resist, pair, weights, sems):
    levels = fields.shape[0]
    top, sign, first, link = order(levels)
    chunk = levels // 4
    early = [
        pltpu.make_async_copy(state.at[:, field], fields.at[:, field], sems.at[8 + i]) for i, field in enumerate((3, 1))
    ]
    early.append(pltpu.make_async_copy(metric, own_metric, sems.at[10]))
    late = [
        pltpu.make_async_copy(state.at[:, field], fields.at[:, field], sems.at[11 + i]) for i, field in enumerate((0, 2))
    ]
    copies = []
    for j in range(4):
        at = pl.ds(top * (levels - chunk) + sign * (j * chunk), chunk)
        copies.append(
            [
                pltpu.make_async_copy(couple.at[at], pair.at[at], sems.at[2 * j]),
                pltpu.make_async_copy(base.at[at], weights.at[at], sems.at[2 * j + 1]),
            ]
        )
    for copy in early + [copy for group in copies for copy in group] + late:
        copy.start()

    for copy in early:
        copy.wait()
    block = block_of(16)
    for half in range(2):

        def gather(i, carry):
            kept_p, kept_v = carry
            moved = []
            for j in range(16):
                at = 16 * i + j
                level = half * (levels // 2) + at
                moved.append(
                    (block == at, pltpu.roll(fields[level, 3], 4 * at, 1), pltpu.roll(fields[level, 1], 4 * at, 1))
                )
            for mine, p, v in moved:
                kept_p = jnp.where(mine, p, kept_p)
                kept_v = jnp.where(mine, v, kept_v)
            return kept_p, kept_v

        kept = jnp.zeros((16, 128), f32)
        kept_p, kept_v = lax.fori_loop(0, levels // 32, gather, (kept, kept))
        edges[16 * half : 16 * half + 16, :] = kept_p
        edges[32 + 16 * half : 48 + 16 * half, :] = kept_v
    own = jnp.where(block == 0, own_metric[...], 0.0)
    for shift in (4, 8, 16, 32, 64):
        own = own + pltpu.roll(own, shift, 1)
    edges[64:80, :] = own
    place = lax.rem(lane_ids(16) + 2, 4)
    for half in range(2):
        at = 16 * half
        p = edges[at : at + 16, :]
        v = edges[32 + at : 48 + at, :]
        sides[0, at : at + 16, :] = jnp.where(
            place < 2, p, jnp.where(place == 2, pltpu.roll(v, 1, 1), pltpu.roll(own, 2, 1))
        )
        sides[1, at : at + 16, :] = jnp.where(
            place >= 2, p, jnp.where(place == 1, pltpu.roll(v, 127, 1), pltpu.roll(own, 126, 1))
        )

    def step(k, carry):
        g, before = carry
        here = first + sign * k
        weight = weights[here]
        after = pair[link + sign * k]
        total = weight + before * g
        inverse = 1.0 / (total + after)
        part_a[here] = weight * inverse
        part_b[here] = before * inverse
        part_c[here] = after * inverse
        return total * inverse, after

    zeros = jnp.zeros((4, 16, 128), f32)
    carry = (zeros, zeros)
    for j in range(4):
        if j == 0:
            for copy in copies[0] + copies[1]:
                copy.wait()
        elif j < 3:
            for copy in copies[j + 1]:
                copy.wait()
        count = chunk if j < 3 else chunk - 1
        start = j * chunk
        if count % 8 == 0:
            carry = loop(count, lambda k, c: step(start + k, c), carry, 8)
        else:
            carry = loop(count, lambda k, c: step(start + k, c), carry, 5)
    g, before = carry
    here = first + sign * (levels - 1)
    weight = weights[here]
    inverse = 1.0 / (weight + before * g)
    part_a[here] = weight * inverse
    part_b[here] = before * inverse
    part_c[here] = inverse
    outward = jnp.where(top == 0, 1.0 / pair[levels - 1], zeros)
    resist[...] = inverse + outward
    for copy in late:
        copy.wait()


def pack_y(sides, low_halo, high_halo, on_chip, off_chip, ends):
    levels = (low_halo.shape[0] - 8) // 3
    block = block_of(8)
    row = row_ids(8)
    kept = jnp.zeros((8, 128), f32)
    for half in range(2):

        def gather(i, kept):
            moved = []
            for j in range(32):
                at = 32 * i + j
                level = half * (levels // 2) + at
                low = jnp.broadcast_to(low_halo[pl.ds(level, 1), :], (8, 128))
                high = jnp.broadcast_to(high_halo[pl.ds(level, 1), :], (8, 128))
                both = pltpu.roll(jnp.where(row == 2 * half, low, high), 4 * at, 1)
                moved.append(((block == at) & (row // 2 == half), both))
            for mine, both in moved:
                kept = jnp.where(mine, both, kept)
            return kept

        kept = lax.fori_loop(0, levels // 64, gather, kept)
    odd = lax.rem(lax.axis_index("gy"), 2)
    for out, side in ((on_chip, odd), (off_chip, 1 - odd)):
        out[0:32, :] = sides[side]
        out[32:40, :] = kept
    ends[...] = kept


def interior(fields, low_halo, high_halo, metric, part_a, part_b, done, reach):
    levels = fields.shape[0]
    top, sign, first, link = order(levels)
    row = row_ids(16)
    m = metric[...]
    slope = step_dt * 0.5 * m
    spread = 0.5 * step_dt * sound_sq * m * m
    slope_low = step_dt * 0.5 * low_halo[3 * levels : 3 * levels + 1, :]
    slope_high = step_dt * 0.5 * high_halo[3 * levels : 3 * levels + 1, :]
    batch = 8

    def east(z):
        return pltpu.roll(z, 127, 1)

    def west(z):
        return pltpu.roll(z, 1, 1)

    def below(z, edge):
        return jnp.where(row == 0, edge, pltpu.roll(z, 1, 0))

    def above(z, edge):
        return jnp.where(row == 15, edge, pltpu.roll(z, 15, 0))

    def several(i, d):
        ls = [first + sign * (i * batch + j) for j in range(batch)]
        pieces = []
        for l in ls:
            pieces.append(
                (
                    fields[l, 3],
                    fields[l, 0],
                    fields[l, 1],
                    low_halo[pl.ds(l, 1), :],
                    low_halo[pl.ds(levels + l, 1), :],
                    low_halo[pl.ds(2 * levels + l, 1), :],
                    high_halo[pl.ds(l, 1), :],
                    high_halo[pl.ds(levels + l, 1), :],
                    high_halo[pl.ds(2 * levels + l, 1), :],
                    [part_a[l, f] for f in range(4)],
                    [part_b[l, f] for f in range(4)],
                    fields[l, 2],
                )
            )
        results = []
        for p, u, v, near_low, far_low, u_low, near_high, far_high, u_high, a, b, w in pieces:
            before = below(p, near_low)
            after = above(p, near_high)
            sides = before + after
            outer = below(before, far_low) + above(after, far_high)
            p_east, p_west = east(p), west(p)
            u1 = u - slope * (after - before)
            v1 = v - slope * (p_east - p_west)
            u1_low = u_low - slope_low * (p[0:1] - far_low)
            u1_high = u_high - slope_high * (far_high - p[15:16])
            diff_u = above(u1, u1_high) - below(u1, u1_low)
            diff_v = east(v1) - west(v1)
            inner = (p_east + p_west) + 2.0 * sides - 8.0 * p
            second = outer + (east(inner) + west(inner)) - 8.0 * sides + 18.0 * p
            p1 = p - spread * (diff_u + diff_v) - hyper_nu * second
            results.append(([a[f] * z for f, z in enumerate((u1, v1, w, p1))], b))
        for l, (drive, b) in zip(ls, results):
            d = tuple(drive[f] + b[f] * d[f] for f in range(4))
            for f in range(4):
                done[l, f] = d[f]
        return d

    zeros = jnp.zeros((16, 128), f32)
    lax.fori_loop(0, levels // batch, several, (zeros,) * 4)

    block = block_of(16)

    reach_batch = 32

    def segment(half, onward):
        def gather(i, carry):
            (on_v, on_p), (kept_v, kept_p) = carry
            moved = []
            for j in range(reach_batch):
                k = levels - 1 - ((1 - half) * (levels // 2) + i * reach_batch + j)
                l = first + sign * k
                at = lax.rem(l, levels // 2)
                moved.append(
                    (block == at, pltpu.roll(part_a[l, 1] * on_v, 4 * at, 1), pltpu.roll(part_a[l, 3] * on_p, 4 * at, 1))
                )
                on_v = part_b[l, 1] * on_v
                on_p = part_b[l, 3] * on_p
            for mine, v, p in moved:
                kept_v = jnp.where(mine, v, kept_v)
                kept_p = jnp.where(mine, p, kept_p)
            return (on_v, on_p), (kept_v, kept_p)

        onward, kept = lax.fori_loop(0, levels // (2 * reach_batch), gather, (onward, (zeros, zeros)))
        at = half + top * (1 - 2 * half)
        reach[0, at] = kept[0]
        reach[1, at] = kept[1]
        return onward

    ones = jnp.ones((16, 128), f32)
    segment(0, segment(1, (ones, ones)))


def finish_forward(done, edges, ends, on_chip, off_chip, reach, resist, out, fixes):
    levels = done.shape[0]
    top, sign, first, link = order(levels)
    turn = lax.axis_index("gy")
    odd = lax.rem(turn, 2) == 1
    near_side, far_side = on_chip[...], off_chip[...]
    left = jnp.where(turn == 0, 0.0, jnp.where(odd, near_side, far_side))
    right = jnp.where(turn == lax.axis_size("gy") - 1, 0.0, jnp.where(odd, far_side, near_side))
    lane = lane_ids(16)
    row = row_ids(16)
    place = lax.rem(lane + 2, 4)
    m = edges[64:80, :]
    slope = step_dt * 0.5 * m
    spread = 0.5 * step_dt * sound_sq * m * m

    def shift(z, by):
        return pltpu.roll(z, by % 128, 1)

    for half in range(2):
        at = 16 * half

        def sides_of(side):
            p = side[at : at + 16, :] - edges[at : at + 16, :]
            low = side[32 + 2 * half : 33 + 2 * half, :] - ends[2 * half : 2 * half + 1, :]
            high = side[33 + 2 * half : 34 + 2 * half, :] - ends[2 * half + 1 : 2 * half + 2, :]
            before = jnp.where(row == 0, low, pltpu.roll(p, 1, 0))
            after = jnp.where(row == 15, high, pltpu.roll(p, 15, 0))
            return p, 2.0 * (before + after) - 8.0 * p

        p_own = edges[at : at + 16, :]
        p_left, cross_left = sides_of(left)
        p_right, cross_right = sides_of(right)
        p_east, p_west = shift(p_own, -1), shift(p_own, 1)
        v1_own = edges[32 + at : 48 + at, :] - slope * (p_east - p_west)
        from_left, from_right = left[at : at + 16, :], right[at : at + 16, :]
        slope_left = step_dt * 0.5 * shift(from_left, -2)
        slope_right = step_dt * 0.5 * shift(from_right, 2)
        v1_left = shift(from_left, -1) - slope_left * (p_east - shift(from_left, 1))
        v1_right = shift(from_right, 1) - slope_right * (shift(from_right, -1) - p_west)
        second = (
            jnp.where(place >= 2, shift(p_left, 2), shift(p_right, -2))
            + jnp.where(place == 2, shift(cross_left, 1), 0.0)
            + jnp.where(place == 1, shift(cross_right, -1), 0.0)
        )
        own_v = jnp.where(
            place == 2, slope * shift(p_left, 1), jnp.where(place == 1, -slope * shift(p_right, -1), 0.0)
        )
        diff_v = jnp.where(
            place == 2,
            shift(v1_own - v1_left, 1),
            jnp.where(
                place == 3,
                -shift(own_v, 1),
                jnp.where(place == 1, shift(v1_right - v1_own, -1), shift(own_v, -1)),
            ),
        )
        fix_p = -spread * diff_v - hyper_nu * second
        fixes[0, half] = own_v
        fixes[1, half] = fix_p
        sum_v = reach[0, half] * own_v + (sum_v if half else 0.0)
        sum_p = reach[1, half] * fix_p + (sum_p if half else 0.0)

    for by in (4, 8, 16, 32, 64):
        sum_v = sum_v + shift(sum_v, by)
        sum_p = sum_p + shift(sum_p, by)
    edge = (lane >= 126) | (lane < 2)
    last = done[first + sign * (levels - 1)]
    out[0, 0] = last[0]
    out[0, 1] = last[1] + jnp.where(edge, sum_v, 0.0)
    out[0, 2] = last[2]
    out[0, 3] = last[3] + jnp.where(edge, sum_p, 0.0)
    out[1] = resist[...]


def settle(before, part_a, part_b, fixes, done):
    levels = before.shape[0]
    top, sign, first, link = order(levels)
    lane = lane_ids(16)
    edge = (lane >= 126) | (lane < 2)
    batch = 16

    def segment(turn, carry):
        half = top + sign * turn
        all_v = fixes[0, half]
        all_p = fixes[1, half]

        def several(i, carry):
            e_v, e_p = carry
            ls = [first + sign * (turn * (levels // 2) + i * batch + j) for j in range(batch)]
            drives = []
            for l in ls:
                back = lax.rem(128 - 4 * (l - half * (levels // 2)), 128)
                v1 = jnp.where(edge, pltpu.roll(all_v, back, 1), 0.0)
                p1 = jnp.where(edge, pltpu.roll(all_p, back, 1), 0.0)
                drives.append(
                    (part_a[l, 1] * v1, part_b[l, 1], part_a[l, 3] * p1, part_b[l, 3], before[l, 1], before[l, 3])
                )
            for l, (drive_v, b_v, drive_p, b_p, d_v, d_p) in zip(ls, drives):
                e_v = drive_v + b_v * e_v
                e_p = drive_p + b_p * e_p
                done[l, 1] = d_v + e_v
                done[l, 3] = d_p + e_p
            return e_v, e_p

        return lax.fori_loop(0, levels // (2 * batch), several, carry)

    zeros = jnp.zeros((16, 128), f32)
    segment(1, segment(0, (zeros, zeros)))


def back_substitute(done, part_c, mine, other, out, x_ref, sems):
    levels = done.shape[0]
    top, sign, first, link = order(levels)
    last = first + sign * (levels - 1)
    x = mine[0] + (other[0] - mine[0]) * (part_c[last] / (mine[1] + other[1]))
    x_ref[last] = x
    chunk = levels // 8
    copies = []

    def several(ks, x):
        ls = [last - sign * k for k in ks]
        loaded = [(part_c[l], done[l]) for l in ls]
        for l, (c, d) in zip(ls, loaded):
            x = d + c * x
            x_ref[l] = x
        return x

    for j in range(8):
        ks = list(range(j * chunk + (j == 0), (j + 1) * chunk))
        for i in range(0, len(ks), 2):
            x = several(ks[i : i + 2], x)
        at = pl.ds((1 - top) * (levels - chunk) - sign * (j * chunk), chunk)
        copy = pltpu.make_async_copy(x_ref.at[at], out.at[at], sems.at[j])
        copy.start()
        copies.append(copy)
    for copy in copies:
        copy.wait()


def near(shape):
    return pltpu.VMEM(shape, f32)


def plain(shape):
    return jax.ShapeDtypeStruct(shape, f32)


def call(body, ins, outs, scratch=(), cost=0, name=None, aliases=None):
    def run(*args):
        return pl.pallas_call(
            body,
            in_specs=ins,
            out_specs=[VM] * len(outs),
            out_shape=outs,
            scratch_shapes=list(scratch),
            name=name,
            input_output_aliases=aliases or {},
            cost_estimate=pl.CostEstimate(flops=cost, bytes_accessed=cost, transcendentals=0) if cost else None,
            compiler_params=pltpu.CompilerParams(vmem_limit_bytes=LIMIT),
        )(*args)

    return run


def far(x):
    return pltpu.with_memory_space_constraint(x, pltpu.HBM)


def shards(state, metric, couple, base):
    levels = state.shape[0]
    nx, ny = lax.axis_size("gx"), lax.axis_size("gy")
    dma = pltpu.SemaphoreType.DMA
    side = (3 * levels + 8, 128)
    full = (levels, 4, 16, 128)
    state, metric, couple, base = far(state), far(metric), far(couple), far(base)

    low_side, high_side = call(
        pack_x, [HB, HB], [plain(side), plain(side)], [dma((8,))], name="pack_x"
    )(state, metric)
    low_halo = lax.ppermute(high_side, "gx", [(i, (i + 1) % nx) for i in range(nx)])
    high_halo = lax.ppermute(low_side, "gx", [((i + 1) % nx, i) for i in range(nx)])

    fields, own_metric, part_a, part_b, part_c, edges, sides, resist = call(
        factor,
        [HB, HB, HB, HB],
        [near(full), near((16, 128)), near(full), near(full), near(full), near((80, 128)), near((2, 32, 128)), near((4, 16, 128))],
        [pltpu.VMEM(full, f32), pltpu.VMEM(full, f32), dma((13,))],
        cost=8 * 1024 * 1024,
        name="factor",
    )(state, couple, base, metric)

    part = (40, 128)
    on_chip, off_chip, ends = call(
        pack_y, [VM] * 3, [plain(part), plain(part), near((8, 128))], name="pack_y"
    )(sides, low_halo, high_halo)
    swaps = []
    for i in range(nx):
        for j in range(ny):
            there = (i ^ 1, j) if j in (0, ny - 1) else (i, j + 1 if j % 2 else j - 1)
            swaps.append((i * ny + j, there[0] * ny + there[1]))
    off_chip = lax.ppermute(off_chip, ("gx", "gy"), swaps)
    on_chip = lax.ppermute(on_chip, "gy", [(j, j ^ 1) for j in range(ny)])

    edge = (2, 2, 16, 128)
    done, reach = call(
        interior,
        [VM] * 6,
        [near(full), near(edge)],
        cost=8 * 1024 * 1024,
        name="interior",
    )(fields, low_halo, high_halo, own_metric, part_a, part_b)

    mine, fixes = call(
        finish_forward,
        [VM] * 7,
        [plain((2, 4, 16, 128)), near(edge)],
        name="finish_forward",
    )(done, edges, ends, on_chip, off_chip, reach, resist)
    other = lax.ppermute(mine, "gz", [(0, 1), (1, 0)])

    done = call(
        settle,
        [VM] * 4,
        [near(full)],
        cost=8 * 1024 * 1024,
        name="settle",
        aliases={0: 0},
    )(done, part_a, part_b, fixes)[0]

    return pl.pallas_call(
        back_substitute,
        in_specs=[VM] * 4,
        out_specs=pl.BlockSpec(memory_space=pl.ANY),
        out_shape=plain(full),
        scratch_shapes=[pltpu.VMEM(full, f32), dma((8,))],
        name="back_substitute",
        compiler_params=pltpu.CompilerParams(vmem_limit_bytes=LIMIT),
    )(done, part_c, mine, other)


def solution(mesh):
    in_specs = (
        P("gz", None, "gx", "gy"),
        P("gx", "gy"),
        P("gz", None, "gx", "gy"),
        P("gz", None, "gx", "gy"),
    )
    out_specs = P("gz", None, "gx", "gy")
    return jax.shard_map(shards, mesh=mesh, in_specs=in_specs, out_specs=out_specs, check_vma=False)
```

```python
import functools

import jax
import jax.numpy as jnp
from jax import lax
from jax.experimental import pallas as pl
from jax.experimental.pallas import tpu as pltpu
from jax.sharding import PartitionSpec as P

step_dt = 0.5
sound_sq = 1.0
hyper_nu = 0.01

f32 = jnp.float32
HB = pl.BlockSpec(memory_space=pltpu.HBM)
VM = pl.BlockSpec(memory_space=pltpu.VMEM)
LIMIT = 32 * 1024 * 1024


def loop(count, body, carry, unroll):
    assert count % unroll == 0

    def several(i, carry):
        for j in range(unroll):
            carry = body(i * unroll + j, carry)
        return carry

    return lax.fori_loop(0, count // unroll, several, carry)


def row_ids(rows):
    return lax.broadcasted_iota(jnp.int32, (rows, 128), 0)


def lane_ids(rows):
    return lax.broadcasted_iota(jnp.int32, (rows, 128), 1)


def order(levels):
    top = lax.axis_index("gz")
    sign = 1 - 2 * top
    return top, sign, top * (levels - 1), top * (levels - 2)


def pack_x(state, metric, low_side, high_side, sems):
    levels = state.shape[0]
    copies = []
    for out, rows in ((low_side, (0, 1, 0)), (high_side, (15, 14, 15))):
        for part, (field, row) in enumerate(zip((3, 3, 0), rows)):
            copies.append((state.at[:, field, row], out.at[pl.ds(part * levels, levels)]))
        copies.append((metric.at[pl.ds(rows[0], 1)], out.at[pl.ds(3 * levels, 1)]))
    copies = [pltpu.make_async_copy(src, dst, sems.at[i]) for i, (src, dst) in enumerate(copies)]
    for copy in copies:
        copy.start()
    for copy in copies:
        copy.wait()


def block_of(rows):
    return lax.rem(lane_ids(rows) + 2, 128) // 4


def factor(state, couple, base, metric, fields, own_metric, part_a, part_b, part_c, edges, sides, resist, pair, weights, sems):
    levels = fields.shape[0]
    top, sign, first, link = order(levels)
    chunk = levels // 4
    early = [
        pltpu.make_async_copy(state.at[:, field], fields.at[:, field], sems.at[8 + i]) for i, field in enumerate((3, 1))
    ]
    early.append(pltpu.make_async_copy(metric, own_metric, sems.at[10]))
    late = [
        pltpu.make_async_copy(state.at[:, field], fields.at[:, field], sems.at[11 + i]) for i, field in enumerate((0, 2))
    ]
    copies = []
    for j in range(4):
        at = pl.ds(top * (levels - chunk) + sign * (j * chunk), chunk)
        copies.append(
            [
                pltpu.make_async_copy(couple.at[at], pair.at[at], sems.at[2 * j]),
                pltpu.make_async_copy(base.at[at], weights.at[at], sems.at[2 * j + 1]),
            ]
        )
    for copy in early + [copy for group in copies for copy in group] + late:
        copy.start()

    block = block_of(16)
    half_levels = levels // 2

    def step(k, carry):
        inflow, before, kept_p, kept_v = carry
        here = first + sign * k
        weight = weights[here]
        after = pair[link + sign * k]
        p, v = fields[here, 3], fields[here, 1]
        inverse = 1.0 / ((weight + after) + inflow)
        pushed = after * (weight + inflow)
        at = lax.rem(here, half_levels)
        mine = block == at
        kept_p = jnp.where(mine, pltpu.roll(p, 4 * at, 1), kept_p)
        kept_v = jnp.where(mine, pltpu.roll(v, 4 * at, 1), kept_v)
        part_a[here] = weight * inverse
        part_b[here] = before * inverse
        part_c[here] = after * inverse
        return pushed * inverse, after, kept_p, kept_v

    for copy in early:
        copy.wait()
    zeros = jnp.zeros((4, 16, 128), f32)
    empty = jnp.zeros((16, 128), f32)
    carry = (zeros, zeros, empty, empty)
    for j in range(4):
        if j == 0:
            for copy in copies[0] + copies[1]:
                copy.wait()
        elif j < 3:
            for copy in copies[j + 1]:
                copy.wait()
        start = j * chunk
        count = chunk if j < 3 else chunk // 2
        carry = loop(count, lambda k, c: step(start + k, c), carry, 8)
        if j == 3:
            for k in range(start + count, levels - 1):
                carry = step(k, carry)
            inflow, before, kept_p, kept_v = carry
            here = first + sign * (levels - 1)
            at = lax.rem(here, half_levels)
            kept_p = jnp.where(block == at, pltpu.roll(fields[here, 3], 4 * at, 1), kept_p)
            kept_v = jnp.where(block == at, pltpu.roll(fields[here, 1], 4 * at, 1), kept_v)
            weight = weights[here]
            inverse = 1.0 / (weight + inflow)
            part_a[here] = weight * inverse
            part_b[here] = before * inverse
            part_c[here] = inverse
            carry = (inflow, before, kept_p, kept_v)
        if j % 2:
            half = top + sign * (j // 2)
            rows = pl.multiple_of(16 * half, 16)
            edges[pl.ds(rows, 16), :] = carry[2]
            edges[pl.ds(32 + rows, 16), :] = carry[3]
            carry = (carry[0], carry[1], empty, empty)
    outward = jnp.where(top == 0, 1.0 / pair[levels - 1], zeros)
    resist[...] = inverse + outward

    own = jnp.where(block == 0, own_metric[...], 0.0)
    for shift in (4, 8, 16, 32, 64):
        own = own + pltpu.roll(own, shift, 1)
    edges[64:80, :] = own
    place = lax.rem(lane_ids(16) + 2, 4)
    for half in range(2):
        at = 16 * half
        p = edges[at : at + 16, :]
        v = edges[32 + at : 48 + at, :]
        sides[0, at : at + 16, :] = jnp.where(
            place < 2, p, jnp.where(place == 2, pltpu.roll(v, 1, 1), pltpu.roll(own, 2, 1))
        )
        sides[1, at : at + 16, :] = jnp.where(
            place >= 2, p, jnp.where(place == 1, pltpu.roll(v, 127, 1), pltpu.roll(own, 126, 1))
        )
    for copy in late:
        copy.wait()


def pack_y(sides, low_halo, high_halo, on_chip, off_chip, ends):
    levels = (low_halo.shape[0] - 8) // 3
    block = block_of(8)
    row = row_ids(8)
    kept = jnp.zeros((8, 128), f32)
    for half in range(2):

        def gather(i, kept):
            moved = []
            for j in range(32):
                at = 32 * i + j
                level = half * (levels // 2) + at
                low = jnp.broadcast_to(low_halo[pl.ds(level, 1), :], (8, 128))
                high = jnp.broadcast_to(high_halo[pl.ds(level, 1), :], (8, 128))
                both = pltpu.roll(jnp.where(row == 2 * half, low, high), 4 * at, 1)
                moved.append(((block == at) & (row // 2 == half), both))
            for mine, both in moved:
                kept = jnp.where(mine, both, kept)
            return kept

        kept = lax.fori_loop(0, levels // 64, gather, kept)
    odd = lax.rem(lax.axis_index("gy"), 2)
    for out, side in ((on_chip, odd), (off_chip, 1 - odd)):
        out[0:32, :] = sides[side]
        out[32:40, :] = kept
    ends[...] = kept


def interior(fields, low_halo, high_halo, metric, part_a, part_b, done, reach):
    levels = fields.shape[0]
    top, sign, first, link = order(levels)
    row = row_ids(16)
    m = metric[...]
    slope = step_dt * 0.5 * m
    spread = 0.5 * step_dt * sound_sq * m * m
    slope_low = step_dt * 0.5 * low_halo[3 * levels : 3 * levels + 1, :]
    slope_high = step_dt * 0.5 * high_halo[3 * levels : 3 * levels + 1, :]
    batch = 4

    def east(z):
        return pltpu.roll(z, 127, 1)

    def west(z):
        return pltpu.roll(z, 1, 1)

    def below(z, edge):
        return jnp.where(row == 0, edge, pltpu.roll(z, 1, 0))

    def above(z, edge):
        return jnp.where(row == 15, edge, pltpu.roll(z, 15, 0))

    def several(i, d):
        ls = [first + sign * (i * batch + j) for j in range(batch)]
        pieces = []
        for l in ls:
            pieces.append(
                (
                    fields[l, 3],
                    fields[l, 0],
                    fields[l, 1],
                    low_halo[pl.ds(l, 1), :],
                    low_halo[pl.ds(levels + l, 1), :],
                    low_halo[pl.ds(2 * levels + l, 1), :],
                    high_halo[pl.ds(l, 1), :],
                    high_halo[pl.ds(levels + l, 1), :],
                    high_halo[pl.ds(2 * levels + l, 1), :],
                    [part_a[l, f] for f in range(4)],
                    [part_b[l, f] for f in range(4)],
                    fields[l, 2],
                )
            )
        results = []
        for p, u, v, near_low, far_low, u_low, near_high, far_high, u_high, a, b, w in pieces:
            before = below(p, near_low)
            after = above(p, near_high)
            sides = before + after
            outer = below(before, far_low) + above(after, far_high)
            p_east, p_west = east(p), west(p)
            u1 = u - slope * (after - before)
            v1 = v - slope * (p_east - p_west)
            u1_low = u_low - slope_low * (p[0:1] - far_low)
            u1_high = u_high - slope_high * (far_high - p[15:16])
            diff_u = above(u1, u1_high) - below(u1, u1_low)
            diff_v = east(v1) - west(v1)
            inner = (p_east + p_west) + 2.0 * sides - 8.0 * p
            second = outer + (east(inner) + west(inner)) - 8.0 * sides + 18.0 * p
            p1 = p - spread * (diff_u + diff_v) - hyper_nu * second
            results.append(([a[f] * z for f, z in enumerate((u1, v1, w, p1))], b))
        for l, (drive, b) in zip(ls, results):
            d = tuple(drive[f] + b[f] * d[f] for f in range(4))
            for f in range(4):
                done[l, f] = d[f]
        return d

    zeros = jnp.zeros((16, 128), f32)
    loop(levels // batch, several, (zeros,) * 4, 2)

    block = block_of(16)

    reach_batch = 32

    def segment(half, onward):
        def gather(i, carry):
            (on_v, on_p), (kept_v, kept_p) = carry
            moved = []
            for j in range(reach_batch):
                k = levels - 1 - ((1 - half) * (levels // 2) + i * reach_batch + j)
                l = first + sign * k
                at = lax.rem(l, levels // 2)
                moved.append(
                    (block == at, pltpu.roll(part_a[l, 1] * on_v, 4 * at, 1), pltpu.roll(part_a[l, 3] * on_p, 4 * at, 1))
                )
                on_v = part_b[l, 1] * on_v
                on_p = part_b[l, 3] * on_p
            for mine, v, p in moved:
                kept_v = jnp.where(mine, v, kept_v)
                kept_p = jnp.where(mine, p, kept_p)
            return (on_v, on_p), (kept_v, kept_p)

        onward, kept = lax.fori_loop(0, levels // (2 * reach_batch), gather, (onward, (zeros, zeros)))
        at = half + top * (1 - 2 * half)
        reach[0, at] = kept[0]
        reach[1, at] = kept[1]
        return onward

    ones = jnp.ones((16, 128), f32)
    segment(0, segment(1, (ones, ones)))


def finish_forward(done, edges, ends, off_chip, on_chip, reach, resist, out, fixes):
    levels = done.shape[0]
    top, sign, first, link = order(levels)
    turn = lax.axis_index("gy")
    odd = lax.rem(turn, 2) == 1
    near_side, far_side = on_chip[...], off_chip[...]
    left = jnp.where(turn == 0, 0.0, jnp.where(odd, near_side, far_side))
    right = jnp.where(turn == lax.axis_size("gy") - 1, 0.0, jnp.where(odd, far_side, near_side))
    lane = lane_ids(16)
    row = row_ids(16)
    place = lax.rem(lane + 2, 4)
    m = edges[64:80, :]
    slope = step_dt * 0.5 * m
    spread = 0.5 * step_dt * sound_sq * m * m

    def shift(z, by):
        return pltpu.roll(z, by % 128, 1)

    for half in range(2):
        at = 16 * half

        def sides_of(side):
            p = side[at : at + 16, :] - edges[at : at + 16, :]
            low = side[32 + 2 * half : 33 + 2 * half, :] - ends[2 * half : 2 * half + 1, :]
            high = side[33 + 2 * half : 34 + 2 * half, :] - ends[2 * half + 1 : 2 * half + 2, :]
            before = jnp.where(row == 0, low, pltpu.roll(p, 1, 0))
            after = jnp.where(row == 15, high, pltpu.roll(p, 15, 0))
            return p, 2.0 * (before + after) - 8.0 * p

        p_own = edges[at : at + 16, :]
        p_left, cross_left = sides_of(left)
        p_right, cross_right = sides_of(right)
        p_east, p_west = shift(p_own, -1), shift(p_own, 1)
        v1_own = edges[32 + at : 48 + at, :] - slope * (p_east - p_west)
        from_left, from_right = left[at : at + 16, :], right[at : at + 16, :]
        slope_left = step_dt * 0.5 * shift(from_left, -2)
        slope_right = step_dt * 0.5 * shift(from_right, 2)
        v1_left = shift(from_left, -1) - slope_left * (p_east - shift(from_left, 1))
        v1_right = shift(from_right, 1) - slope_right * (shift(from_right, -1) - p_west)
        second = (
            jnp.where(place >= 2, shift(p_left, 2), shift(p_right, -2))
            + jnp.where(place == 2, shift(cross_left, 1), 0.0)
            + jnp.where(place == 1, shift(cross_right, -1), 0.0)
        )
        own_v = jnp.where(
            place == 2, slope * shift(p_left, 1), jnp.where(place == 1, -slope * shift(p_right, -1), 0.0)
        )
        diff_v = jnp.where(
            place == 2,
            shift(v1_own - v1_left, 1),
            jnp.where(
                place == 3,
                -shift(own_v, 1),
                jnp.where(place == 1, shift(v1_right - v1_own, -1), shift(own_v, -1)),
            ),
        )
        fix_p = -spread * diff_v - hyper_nu * second
        fixes[0, half] = own_v
        fixes[1, half] = fix_p
        sum_v = reach[0, half] * own_v + (sum_v if half else 0.0)
        sum_p = reach[1, half] * fix_p + (sum_p if half else 0.0)

    for steps in ((4, 8, 12, 16, 20, 24, 28), (32, 64, 96)):
        sum_v = sum([shift(sum_v, by) for by in steps], sum_v)
        sum_p = sum([shift(sum_p, by) for by in steps], sum_p)
    edge = (lane >= 126) | (lane < 2)
    last = done[first + sign * (levels - 1)]
    out[0, 0] = last[0]
    out[0, 1] = last[1] + jnp.where(edge, sum_v, 0.0)
    out[0, 2] = last[2]
    out[0, 3] = last[3] + jnp.where(edge, sum_p, 0.0)
    out[1] = resist[...]


def settle(before, part_a, part_b, fixes, done):
    levels = before.shape[0]
    top, sign, first, link = order(levels)
    lane = lane_ids(16)
    edge = (lane >= 126) | (lane < 2)
    batch = 16

    def segment(turn, carry):
        half = top + sign * turn
        all_v = fixes[0, half]
        all_p = fixes[1, half]

        def several(i, carry):
            e_v, e_p = carry
            ls = [first + sign * (turn * (levels // 2) + i * batch + j) for j in range(batch)]
            drives = []
            for l in ls:
                back = lax.rem(128 - 4 * (l - half * (levels // 2)), 128)
                v1 = jnp.where(edge, pltpu.roll(all_v, back, 1), 0.0)
                p1 = jnp.where(edge, pltpu.roll(all_p, back, 1), 0.0)
                drives.append(
                    (part_a[l, 1] * v1, part_b[l, 1], part_a[l, 3] * p1, part_b[l, 3], before[l, 1], before[l, 3])
                )
            for l, (drive_v, b_v, drive_p, b_p, d_v, d_p) in zip(ls, drives):
                e_v = drive_v + b_v * e_v
                e_p = drive_p + b_p * e_p
                done[l, 1] = d_v + e_v
                done[l, 3] = d_p + e_p
            return e_v, e_p

        return lax.fori_loop(0, levels // (2 * batch), several, carry)

    zeros = jnp.zeros((16, 128), f32)
    segment(1, segment(0, (zeros, zeros)))


def back_substitute(done, part_c, mine, other, out, x_ref, sems):
    levels = done.shape[0]
    top, sign, first, link = order(levels)
    last = first + sign * (levels - 1)
    x = mine[0] + (other[0] - mine[0]) * (part_c[last] / (mine[1] + other[1]))
    x_ref[last] = x
    chunk = levels // 8
    copies = []

    def several(ks, x):
        ls = [last - sign * k for k in ks]
        loaded = [(part_c[l], done[l]) for l in ls]
        for l, (c, d) in zip(ls, loaded):
            x = d + c * x
            x_ref[l] = x
        return x

    for j in range(8):
        ks = list(range(j * chunk + (j == 0), (j + 1) * chunk))
        for i in range(0, len(ks), 2):
            x = several(ks[i : i + 2], x)
        at = pl.ds((1 - top) * (levels - chunk) - sign * (j * chunk), chunk)
        copy = pltpu.make_async_copy(x_ref.at[at], out.at[at], sems.at[j])
        copy.start()
        copies.append(copy)
    for copy in copies:
        copy.wait()


def near(shape):
    return pltpu.VMEM(shape, f32)


def plain(shape):
    return jax.ShapeDtypeStruct(shape, f32)


def call(body, ins, outs, scratch=(), cost=0, name=None, aliases=None):
    def run(*args):
        return pl.pallas_call(
            body,
            in_specs=ins,
            out_specs=[VM] * len(outs),
            out_shape=outs,
            scratch_shapes=list(scratch),
            name=name,
            input_output_aliases=aliases or {},
            cost_estimate=pl.CostEstimate(flops=cost, bytes_accessed=cost, transcendentals=0) if cost else None,
            compiler_params=pltpu.CompilerParams(vmem_limit_bytes=LIMIT),
        )(*args)

    return run


def far(x):
    return pltpu.with_memory_space_constraint(x, pltpu.HBM)


def shards(state, metric, couple, base):
    levels = state.shape[0]
    nx, ny = lax.axis_size("gx"), lax.axis_size("gy")
    dma = pltpu.SemaphoreType.DMA
    side = (3 * levels + 8, 128)
    full = (levels, 4, 16, 128)
    state, metric, couple, base = far(state), far(metric), far(couple), far(base)

    low_side, high_side = call(
        pack_x, [HB, HB], [plain(side), plain(side)], [dma((8,))], name="pack_x"
    )(state, metric)
    low_halo = lax.ppermute(high_side, "gx", [(i, (i + 1) % nx) for i in range(nx)])
    high_halo = lax.ppermute(low_side, "gx", [((i + 1) % nx, i) for i in range(nx)])

    fields, own_metric, part_a, part_b, part_c, edges, sides, resist = call(
        factor,
        [HB, HB, HB, HB],
        [near(full), near((16, 128)), near(full), near(full), near(full), near((80, 128)), near((2, 32, 128)), near((4, 16, 128))],
        [pltpu.VMEM(full, f32), pltpu.VMEM(full, f32), dma((13,))],
        cost=8 * 1024 * 1024,
        name="factor",
    )(state, couple, base, metric)

    part = (40, 128)
    on_chip, off_chip, ends = call(
        pack_y, [VM] * 3, [plain(part), plain(part), near((8, 128))], name="pack_y"
    )(sides, low_halo, high_halo)
    swaps = []
    for i in range(nx):
        for j in range(ny):
            there = (i ^ 1, j) if j in (0, ny - 1) else (i, j + 1 if j % 2 else j - 1)
            swaps.append((i * ny + j, there[0] * ny + there[1]))
    off_chip = lax.ppermute(off_chip, ("gx", "gy"), swaps)
    on_chip = lax.ppermute(on_chip, "gy", [(j, j ^ 1) for j in range(ny)])

    edge = (2, 2, 16, 128)
    done, reach = call(
        interior,
        [VM] * 6,
        [near(full), near(edge)],
        cost=8 * 1024 * 1024,
        name="interior",
    )(fields, low_halo, high_halo, own_metric, part_a, part_b)

    mine, fixes = call(
        finish_forward,
        [VM] * 7,
        [plain((2, 4, 16, 128)), near(edge)],
        name="finish_forward",
    )(done, edges, ends, off_chip, on_chip, reach, resist)
    other = lax.ppermute(mine, "gz", [(0, 1), (1, 0)])

    done = call(
        settle,
        [VM] * 4,
        [near(full)],
        cost=8 * 1024 * 1024,
        name="settle",
        aliases={0: 0},
    )(done, part_a, part_b, fixes)[0]

    return pl.pallas_call(
        back_substitute,
        in_specs=[VM] * 4,
        out_specs=pl.BlockSpec(memory_space=pl.ANY),
        out_shape=plain(full),
        scratch_shapes=[pltpu.VMEM(full, f32), dma((8,))],
        name="back_substitute",
        compiler_params=pltpu.CompilerParams(vmem_limit_bytes=LIMIT),
    )(done, part_c, mine, other)


def solution(mesh):
    in_specs = (
        P("gz", None, "gx", "gy"),
        P("gx", "gy"),
        P("gz", None, "gx", "gy"),
        P("gz", None, "gx", "gy"),
    )
    out_specs = P("gz", None, "gx", "gy")
    return jax.shard_map(shards, mesh=mesh, in_specs=in_specs, out_specs=out_specs, check_vma=False)
```

```python
import functools

import jax
import jax.numpy as jnp
from jax import lax
from jax.experimental import pallas as pl
from jax.experimental.pallas import tpu as pltpu
from jax.sharding import PartitionSpec as P

step_dt = 0.5
sound_sq = 1.0
hyper_nu = 0.01

f32 = jnp.float32
HB = pl.BlockSpec(memory_space=pltpu.HBM)
VM = pl.BlockSpec(memory_space=pltpu.VMEM)
LIMIT = 32 * 1024 * 1024


def loop(count, body, carry, unroll):
    assert count % unroll == 0

    def several(i, carry):
        for j in range(unroll):
            carry = body(i * unroll + j, carry)
        return carry

    return lax.fori_loop(0, count // unroll, several, carry)


def row_ids(rows):
    return lax.broadcasted_iota(jnp.int32, (rows, 128), 0)


def lane_ids(rows):
    return lax.broadcasted_iota(jnp.int32, (rows, 128), 1)


def order(levels):
    top = lax.axis_index("gz")
    sign = 1 - 2 * top
    return top, sign, top * (levels - 1), top * (levels - 2)


def pack_x(state, metric, low_side, high_side, sems):
    levels = state.shape[0]
    copies = []
    for out, rows in ((low_side, (0, 1, 0)), (high_side, (15, 14, 15))):
        for part, (field, row) in enumerate(zip((3, 3, 0), rows)):
            copies.append((state.at[:, field, row], out.at[pl.ds(part * levels, levels)]))
        copies.append((metric.at[pl.ds(rows[0], 1)], out.at[pl.ds(3 * levels, 1)]))
    copies = [pltpu.make_async_copy(src, dst, sems.at[i]) for i, (src, dst) in enumerate(copies)]
    for copy in copies:
        copy.start()
    for copy in copies:
        copy.wait()


def block_of(rows):
    return lax.rem(lane_ids(rows) + 2, 128) // 4


def factor(state, couple, base, metric, fields, own_metric, part_a, part_b, part_c, edges, sides, resist, pair, weights, sems):
    levels = fields.shape[0]
    top, sign, first, link = order(levels)
    chunk = levels // 4
    early = [
        pltpu.make_async_copy(state.at[:, field], fields.at[:, field], sems.at[8 + i]) for i, field in enumerate((3, 1))
    ]
    early.append(pltpu.make_async_copy(metric, own_metric, sems.at[10]))
    late = [
        pltpu.make_async_copy(state.at[:, field], fields.at[:, field], sems.at[11 + i]) for i, field in enumerate((0, 2))
    ]
    copies = []
    for j in range(4):
        at = pl.ds(top * (levels - chunk) + sign * (j * chunk), chunk)
        copies.append(
            [
                pltpu.make_async_copy(couple.at[at], pair.at[at], sems.at[2 * j]),
                pltpu.make_async_copy(base.at[at], weights.at[at], sems.at[2 * j + 1]),
            ]
        )
    for copy in early + [copy for group in copies for copy in group] + late:
        copy.start()

    block = block_of(16)
    half_levels = levels // 2

    def step(k, carry):
        inflow, before, kept_p, kept_v = carry
        here = first + sign * k
        weight = weights[here]
        after = pair[link + sign * k]
        p, v = fields[here, 3], fields[here, 1]
        inverse = 1.0 / ((weight + after) + inflow)
        pushed = after * (weight + inflow)
        at = lax.rem(here, half_levels)
        mine = block == at
        kept_p = jnp.where(mine, pltpu.roll(p, 4 * at, 1), kept_p)
        kept_v = jnp.where(mine, pltpu.roll(v, 4 * at, 1), kept_v)
        part_a[here] = weight * inverse
        part_b[here] = before * inverse
        part_c[here] = after * inverse
        return pushed * inverse, after, kept_p, kept_v

    for copy in early:
        copy.wait()
    zeros = jnp.zeros((4, 16, 128), f32)
    empty = jnp.zeros((16, 128), f32)
    carry = (zeros, zeros, empty, empty)
    for j in range(4):
        if j == 0:
            for copy in copies[0] + copies[1]:
                copy.wait()
        elif j < 3:
            for copy in copies[j + 1]:
                copy.wait()
        start = j * chunk
        count = chunk if j < 3 else chunk // 2
        carry = loop(count, lambda k, c: step(start + k, c), carry, count)
        if j == 3:
            for k in range(start + count, levels - 1):
                carry = step(k, carry)
            inflow, before, kept_p, kept_v = carry
            here = first + sign * (levels - 1)
            at = lax.rem(here, half_levels)
            kept_p = jnp.where(block == at, pltpu.roll(fields[here, 3], 4 * at, 1), kept_p)
            kept_v = jnp.where(block == at, pltpu.roll(fields[here, 1], 4 * at, 1), kept_v)
            weight = weights[here]
            inverse = 1.0 / (weight + inflow)
            part_a[here] = weight * inverse
            part_b[here] = before * inverse
            part_c[here] = inverse
            carry = (inflow, before, kept_p, kept_v)
        if j % 2:
            half = top + sign * (j // 2)
            rows = pl.multiple_of(16 * half, 16)
            edges[pl.ds(rows, 16), :] = carry[2]
            edges[pl.ds(32 + rows, 16), :] = carry[3]
            carry = (carry[0], carry[1], empty, empty)
    outward = jnp.where(top == 0, 1.0 / pair[levels - 1], zeros)
    resist[...] = inverse + outward

    own = jnp.where(block == 0, own_metric[...], 0.0)
    for shift in (4, 8, 16, 32, 64):
        own = own + pltpu.roll(own, shift, 1)
    edges[64:80, :] = own
    place = lax.rem(lane_ids(16) + 2, 4)
    for half in range(2):
        at = 16 * half
        p = edges[at : at + 16, :]
        v = edges[32 + at : 48 + at, :]
        sides[0, at : at + 16, :] = jnp.where(
            place < 2, p, jnp.where(place == 2, pltpu.roll(v, 1, 1), pltpu.roll(own, 2, 1))
        )
        sides[1, at : at + 16, :] = jnp.where(
            place >= 2, p, jnp.where(place == 1, pltpu.roll(v, 127, 1), pltpu.roll(own, 126, 1))
        )
    for copy in late:
        copy.wait()


def pack_y(sides, low_halo, high_halo, on_chip, off_chip, ends):
    levels = (low_halo.shape[0] - 8) // 3
    block = block_of(8)
    row = row_ids(8)
    kept = jnp.zeros((8, 128), f32)
    for half in range(2):

        def gather(i, kept):
            moved = []
            for j in range(32):
                at = 32 * i + j
                level = half * (levels // 2) + at
                low = jnp.broadcast_to(low_halo[pl.ds(level, 1), :], (8, 128))
                high = jnp.broadcast_to(high_halo[pl.ds(level, 1), :], (8, 128))
                both = pltpu.roll(jnp.where(row == 2 * half, low, high), 4 * at, 1)
                moved.append(((block == at) & (row // 2 == half), both))
            for mine, both in moved:
                kept = jnp.where(mine, both, kept)
            return kept

        kept = lax.fori_loop(0, levels // 64, gather, kept)
    odd = lax.rem(lax.axis_index("gy"), 2)
    for out, side in ((on_chip, odd), (off_chip, 1 - odd)):
        out[0:32, :] = sides[side]
        out[32:40, :] = kept
    ends[...] = kept


def interior(fields, low_halo, high_halo, metric, part_a, part_b, done, reach):
    levels = fields.shape[0]
    top, sign, first, link = order(levels)
    row = row_ids(16)
    m = metric[...]
    slope = step_dt * 0.5 * m
    spread = 0.5 * step_dt * sound_sq * m * m
    spread_first, spread_last = spread[0:1], spread[15:16]
    spread_below, spread_above = pltpu.roll(spread, 1, 0), pltpu.roll(spread, 15, 0)
    spread_west, spread_east = pltpu.roll(spread, 1, 1), pltpu.roll(spread, 127, 1)
    slope_low = step_dt * 0.5 * low_halo[3 * levels : 3 * levels + 1, :]
    slope_high = step_dt * 0.5 * high_halo[3 * levels : 3 * levels + 1, :]
    batch = 16

    def east(z):
        return pltpu.roll(z, 127, 1)

    def west(z):
        return pltpu.roll(z, 1, 1)

    def below(z, edge):
        return jnp.where(row == 0, edge, pltpu.roll(z, 1, 0))

    def above(z, edge):
        return jnp.where(row == 15, edge, pltpu.roll(z, 15, 0))

    def several(i, d):
        ls = [first + sign * (i * batch + j) for j in range(batch)]
        pieces = []
        for l in ls:
            pieces.append(
                (
                    fields[l, 3],
                    fields[l, 0],
                    fields[l, 1],
                    low_halo[pl.ds(l, 1), :],
                    low_halo[pl.ds(levels + l, 1), :],
                    low_halo[pl.ds(2 * levels + l, 1), :],
                    high_halo[pl.ds(l, 1), :],
                    high_halo[pl.ds(levels + l, 1), :],
                    high_halo[pl.ds(2 * levels + l, 1), :],
                    [part_a[l, f] for f in range(4)],
                    [part_b[l, f] for f in range(4)],
                    fields[l, 2],
                )
            )
        results = []
        for p, u, v, near_low, far_low, u_low, near_high, far_high, u_high, a, b, w in pieces:
            before = below(p, near_low)
            after = above(p, near_high)
            sides = before + after
            p_east, p_west = east(p), west(p)
            u1 = u - slope * (after - before)
            v1 = v - slope * (p_east - p_west)
            u1_low = u_low - slope_low * (p[0:1] - far_low)
            u1_high = u_high - slope_high * (far_high - p[15:16])
            inner = hyper_nu * ((p_east + p_west) + 2.0 * sides - 8.0 * p)
            p1 = (
                (1.0 - 18.0 * hyper_nu) * p
                + 8.0 * hyper_nu * sides
                - above(u1 * spread_below + hyper_nu * after, u1_high * spread_last + hyper_nu * far_high)
                + below(u1 * spread_above - hyper_nu * before, u1_low * spread_first - hyper_nu * far_low)
                - east(v1 * spread_west + inner)
                + west(v1 * spread_east - inner)
            )
            results.append(([a[f] * z for f, z in enumerate((u1, v1, w, p1))], b))
        for l, (drive, b) in zip(ls, results):
            d = tuple(drive[f] + b[f] * d[f] for f in range(4))
            for f in range(4):
                done[l, f] = d[f]
        return d

    zeros = jnp.zeros((16, 128), f32)
    loop(levels // batch, several, (zeros,) * 4, 1)

    block = block_of(16)

    reach_batch = 32

    def segment(half, onward):
        def gather(i, carry):
            (on_v, on_p), (kept_v, kept_p) = carry
            moved = []
            for j in range(reach_batch):
                k = levels - 1 - ((1 - half) * (levels // 2) + i * reach_batch + j)
                l = first + sign * k
                at = lax.rem(l, levels // 2)
                moved.append(
                    (block == at, pltpu.roll(part_a[l, 1] * on_v, 4 * at, 1), pltpu.roll(part_a[l, 3] * on_p, 4 * at, 1))
                )
                on_v = part_b[l, 1] * on_v
                on_p = part_b[l, 3] * on_p
            for mine, v, p in moved:
                kept_v = jnp.where(mine, v, kept_v)
                kept_p = jnp.where(mine, p, kept_p)
            return (on_v, on_p), (kept_v, kept_p)

        onward, kept = lax.fori_loop(0, levels // (2 * reach_batch), gather, (onward, (zeros, zeros)))
        at = half + top * (1 - 2 * half)
        reach[0, at] = kept[0]
        reach[1, at] = kept[1]
        return onward

    ones = jnp.ones((16, 128), f32)
    segment(0, segment(1, (ones, ones)))


def finish_forward(done, edges, ends, off_chip, on_chip, reach, resist, out, fixes):
    levels = done.shape[0]
    top, sign, first, link = order(levels)
    turn = lax.axis_index("gy")
    odd = lax.rem(turn, 2) == 1
    near_side, far_side = on_chip[...], off_chip[...]
    left = jnp.where(turn == 0, 0.0, jnp.where(odd, near_side, far_side))
    right = jnp.where(turn == lax.axis_size("gy") - 1, 0.0, jnp.where(odd, far_side, near_side))
    lane = lane_ids(16)
    row = row_ids(16)
    place = lax.rem(lane + 2, 4)
    m = edges[64:80, :]
    slope = step_dt * 0.5 * m
    spread = 0.5 * step_dt * sound_sq * m * m

    def shift(z, by):
        return pltpu.roll(z, by % 128, 1)

    for half in range(2):
        at = 16 * half

        def sides_of(side):
            p = side[at : at + 16, :] - edges[at : at + 16, :]
            low = side[32 + 2 * half : 33 + 2 * half, :] - ends[2 * half : 2 * half + 1, :]
            high = side[33 + 2 * half : 34 + 2 * half, :] - ends[2 * half + 1 : 2 * half + 2, :]
            before = jnp.where(row == 0, low, pltpu.roll(p, 1, 0))
            after = jnp.where(row == 15, high, pltpu.roll(p, 15, 0))
            return p, 2.0 * (before + after) - 8.0 * p

        p_own = edges[at : at + 16, :]
        p_left, cross_left = sides_of(left)
        p_right, cross_right = sides_of(right)
        p_east, p_west = shift(p_own, -1), shift(p_own, 1)
        v1_own = edges[32 + at : 48 + at, :] - slope * (p_east - p_west)
        from_left, from_right = left[at : at + 16, :], right[at : at + 16, :]
        slope_left = step_dt * 0.5 * shift(from_left, -2)
        slope_right = step_dt * 0.5 * shift(from_right, 2)
        v1_left = shift(from_left, -1) - slope_left * (p_east - shift(from_left, 1))
        v1_right = shift(from_right, 1) - slope_right * (shift(from_right, -1) - p_west)
        second = (
            jnp.where(place >= 2, shift(p_left, 2), shift(p_right, -2))
            + jnp.where(place == 2, shift(cross_left, 1), 0.0)
            + jnp.where(place == 1, shift(cross_right, -1), 0.0)
        )
        own_v = jnp.where(
            place == 2, slope * shift(p_left, 1), jnp.where(place == 1, -slope * shift(p_right, -1), 0.0)
        )
        diff_v = jnp.where(
            place == 2,
            shift(v1_own - v1_left, 1),
            jnp.where(
                place == 3,
                -shift(own_v, 1),
                jnp.where(place == 1, shift(v1_right - v1_own, -1), shift(own_v, -1)),
            ),
        )
        fix_p = -spread * diff_v - hyper_nu * second
        fixes[0, half] = own_v
        fixes[1, half] = fix_p
        sum_v = reach[0, half] * own_v + (sum_v if half else 0.0)
        sum_p = reach[1, half] * fix_p + (sum_p if half else 0.0)

    for steps in ((4, 8, 12, 16, 20, 24, 28), (32, 64, 96)):
        sum_v = sum([shift(sum_v, by) for by in steps], sum_v)
        sum_p = sum([shift(sum_p, by) for by in steps], sum_p)
    edge = (lane >= 126) | (lane < 2)
    last = done[first + sign * (levels - 1)]
    out[0, 0] = last[0]
    out[0, 1] = last[1] + jnp.where(edge, sum_v, 0.0)
    out[0, 2] = last[2]
    out[0, 3] = last[3] + jnp.where(edge, sum_p, 0.0)
    out[1] = resist[...]


def settle(before, part_a, part_b, fixes, done):
    levels = before.shape[0]
    top, sign, first, link = order(levels)
    lane = lane_ids(16)
    edge = (lane >= 126) | (lane < 2)
    batch = 16

    def segment(turn, carry):
        half = top + sign * turn
        all_v = fixes[0, half]
        all_p = fixes[1, half]

        def several(i, carry):
            e_v, e_p = carry
            ls = [first + sign * (turn * (levels // 2) + i * batch + j) for j in range(batch)]
            drives = []
            for l in ls:
                back = lax.rem(128 - 4 * (l - half * (levels // 2)), 128)
                v1 = jnp.where(edge, pltpu.roll(all_v, back, 1), 0.0)
                p1 = jnp.where(edge, pltpu.roll(all_p, back, 1), 0.0)
                drives.append(
                    (part_a[l, 1] * v1, part_b[l, 1], part_a[l, 3] * p1, part_b[l, 3], before[l, 1], before[l, 3])
                )
            for l, (drive_v, b_v, drive_p, b_p, d_v, d_p) in zip(ls, drives):
                e_v = drive_v + b_v * e_v
                e_p = drive_p + b_p * e_p
                done[l, 1] = d_v + e_v
                done[l, 3] = d_p + e_p
            return e_v, e_p

        return lax.fori_loop(0, levels // (2 * batch), several, carry)

    zeros = jnp.zeros((16, 128), f32)
    segment(1, segment(0, (zeros, zeros)))


def back_substitute(done, part_c, mine, other, out, x_ref, sems):
    levels = done.shape[0]
    top, sign, first, link = order(levels)
    last = first + sign * (levels - 1)
    x = mine[0] + (other[0] - mine[0]) * (part_c[last] / (mine[1] + other[1]))
    x_ref[last] = x
    chunk = levels // 8
    copies = []

    def several(ks, x):
        ls = [last - sign * k for k in ks]
        loaded = [(part_c[l], done[l]) for l in ls]
        for l, (c, d) in zip(ls, loaded):
            x = d + c * x
            x_ref[l] = x
        return x

    for j in range(8):
        ks = list(range(j * chunk + (j == 0), (j + 1) * chunk))
        for i in range(0, len(ks), 4):
            x = several(ks[i : i + 4], x)
        at = pl.ds((1 - top) * (levels - chunk) - sign * (j * chunk), chunk)
        copy = pltpu.make_async_copy(x_ref.at[at], out.at[at], sems.at[j])
        copy.start()
        copies.append(copy)
    for copy in copies:
        copy.wait()


def near(shape):
    return pltpu.VMEM(shape, f32)


def plain(shape):
    return jax.ShapeDtypeStruct(shape, f32)


def call(body, ins, outs, scratch=(), cost=0, name=None, aliases=None):
    def run(*args):
        return pl.pallas_call(
            body,
            in_specs=ins,
            out_specs=[VM] * len(outs),
            out_shape=outs,
            scratch_shapes=list(scratch),
            name=name,
            input_output_aliases=aliases or {},
            cost_estimate=pl.CostEstimate(flops=cost, bytes_accessed=cost, transcendentals=0) if cost else None,
            compiler_params=pltpu.CompilerParams(vmem_limit_bytes=LIMIT),
        )(*args)

    return run


def far(x):
    return pltpu.with_memory_space_constraint(x, pltpu.HBM)


def shards(state, metric, couple, base):
    levels = state.shape[0]
    nx, ny = lax.axis_size("gx"), lax.axis_size("gy")
    dma = pltpu.SemaphoreType.DMA
    side = (3 * levels + 8, 128)
    full = (levels, 4, 16, 128)
    state, metric, couple, base = far(state), far(metric), far(couple), far(base)

    low_side, high_side = call(
        pack_x, [HB, HB], [plain(side), plain(side)], [dma((8,))], name="pack_x"
    )(state, metric)
    low_halo = lax.ppermute(high_side, "gx", [(i, (i + 1) % nx) for i in range(nx)])
    high_halo = lax.ppermute(low_side, "gx", [((i + 1) % nx, i) for i in range(nx)])

    fields, own_metric, part_a, part_b, part_c, edges, sides, resist = call(
        factor,
        [HB, HB, HB, HB],
        [near(full), near((16, 128)), near(full), near(full), near(full), near((80, 128)), near((2, 32, 128)), near((4, 16, 128))],
        [pltpu.VMEM(full, f32), pltpu.VMEM(full, f32), dma((13,))],
        cost=8 * 1024 * 1024,
        name="factor",
    )(state, couple, base, metric)

    part = (40, 128)
    on_chip, off_chip, ends = call(
        pack_y, [VM] * 3, [plain(part), plain(part), near((8, 128))], name="pack_y"
    )(sides, low_halo, high_halo)
    swaps = []
    for i in range(nx):
        for j in range(ny):
            there = (i ^ 1, j) if j in (0, ny - 1) else (i, j + 1 if j % 2 else j - 1)
            swaps.append((i * ny + j, there[0] * ny + there[1]))
    off_chip = lax.ppermute(off_chip, ("gx", "gy"), swaps)
    on_chip = lax.ppermute(on_chip, "gy", [(j, j ^ 1) for j in range(ny)])

    edge = (2, 2, 16, 128)
    done, reach = call(
        interior,
        [VM] * 6,
        [near(full), near(edge)],
        cost=8 * 1024 * 1024,
        name="interior",
    )(fields, low_halo, high_halo, own_metric, part_a, part_b)

    mine, fixes = call(
        finish_forward,
        [VM] * 7,
        [plain((2, 4, 16, 128)), near(edge)],
        name="finish_forward",
    )(done, edges, ends, off_chip, on_chip, reach, resist)
    other = lax.ppermute(mine, "gz", [(0, 1), (1, 0)])

    done = call(
        settle,
        [VM] * 4,
        [near(full)],
        cost=8 * 1024 * 1024,
        name="settle",
        aliases={0: 0},
    )(done, part_a, part_b, fixes)[0]

    return pl.pallas_call(
        back_substitute,
        in_specs=[VM] * 4,
        out_specs=pl.BlockSpec(memory_space=pl.ANY),
        out_shape=plain(full),
        scratch_shapes=[pltpu.VMEM(full, f32), dma((8,))],
        name="back_substitute",
        compiler_params=pltpu.CompilerParams(vmem_limit_bytes=LIMIT),
    )(done, part_c, mine, other)


def solution(mesh):
    in_specs = (
        P("gz", None, "gx", "gy"),
        P("gx", "gy"),
        P("gz", None, "gx", "gy"),
        P("gz", None, "gx", "gy"),
    )
    out_specs = P("gz", None, "gx", "gy")
    return jax.shard_map(shards, mesh=mesh, in_specs=in_specs, out_specs=out_specs, check_vma=False)
```

```python
import functools

import jax
import jax.numpy as jnp
from jax import lax
from jax.experimental import pallas as pl
from jax.experimental.pallas import tpu as pltpu
from jax.sharding import PartitionSpec as P

step_dt = 0.5
sound_sq = 1.0
hyper_nu = 0.01

f32 = jnp.float32
HB = pl.BlockSpec(memory_space=pltpu.HBM)
VM = pl.BlockSpec(memory_space=pltpu.VMEM)
LIMIT = 32 * 1024 * 1024


def loop(count, body, carry, unroll):
    assert count % unroll == 0

    def several(i, carry):
        for j in range(unroll):
            carry = body(i * unroll + j, carry)
        return carry

    return lax.fori_loop(0, count // unroll, several, carry)


def row_ids(rows):
    return lax.broadcasted_iota(jnp.int32, (rows, 128), 0)


def lane_ids(rows):
    return lax.broadcasted_iota(jnp.int32, (rows, 128), 1)


def order(levels):
    top = lax.axis_index("gz")
    sign = 1 - 2 * top
    return top, sign, top * (levels - 1), top * (levels - 2)


def pack_x(state, metric, low_side, high_side, sems):
    levels = state.shape[0]
    copies = []
    for out, pair, row in ((low_side, 0, 0), (high_side, 14, 15)):
        copies.append((state.at[:, 3, pl.ds(pair, 2)], out.at[pl.ds(0, 2 * levels)].reshape(levels, 2, 128)))
        copies.append((state.at[:, 0, row], out.at[pl.ds(2 * levels, levels)]))
        copies.append((metric.at[pl.ds(row, 1)], out.at[pl.ds(3 * levels, 1)]))
    copies = [pltpu.make_async_copy(src, dst, sems.at[i]) for i, (src, dst) in enumerate(copies)]
    for copy in copies:
        copy.start()
    for copy in copies:
        copy.wait()


def block_of(rows):
    return lax.rem(lane_ids(rows) + 2, 128) // 4


def factor(state, couple, base, metric, fields, own_metric, part_a, part_b, part_c, edges, sides, resist, pair, weights, sems):
    levels = fields.shape[0]
    top, sign, first, link = order(levels)
    chunk = levels // 4
    early = [
        pltpu.make_async_copy(state.at[:, field], fields.at[:, field], sems.at[8 + i]) for i, field in enumerate((3, 1))
    ]
    early.append(pltpu.make_async_copy(metric, own_metric, sems.at[10]))
    late = [
        pltpu.make_async_copy(state.at[:, field], fields.at[:, field], sems.at[11 + i]) for i, field in enumerate((0, 2))
    ]
    copies = []
    for j in range(4):
        at = pl.ds(top * (levels - chunk) + sign * (j * chunk), chunk)
        copies.append(
            [
                pltpu.make_async_copy(couple.at[at], pair.at[at], sems.at[2 * j]),
                pltpu.make_async_copy(base.at[at], weights.at[at], sems.at[2 * j + 1]),
            ]
        )
    for copy in early + [copy for group in copies for copy in group] + late:
        copy.start()

    block = block_of(16)
    half_levels = levels // 2

    def step(k, carry):
        inflow, before, kept_p, kept_v = carry
        here = first + sign * k
        weight = weights[here]
        after = pair[link + sign * k]
        p, v = fields[here, 3], fields[here, 1]
        inverse = 1.0 / ((weight + after) + inflow)
        pushed = after * (weight + inflow)
        at = lax.rem(here, half_levels)
        mine = block == at
        kept_p = jnp.where(mine, pltpu.roll(p, 4 * at, 1), kept_p)
        kept_v = jnp.where(mine, pltpu.roll(v, 4 * at, 1), kept_v)
        part_a[here] = weight * inverse
        part_b[here] = before * inverse
        part_c[here] = after * inverse
        return pushed * inverse, after, kept_p, kept_v

    for copy in early:
        copy.wait()
    zeros = jnp.zeros((4, 16, 128), f32)
    empty = jnp.zeros((16, 128), f32)
    carry = (zeros, zeros, empty, empty)
    for j in range(4):
        if j == 0:
            for copy in copies[0] + copies[1]:
                copy.wait()
        elif j < 3:
            for copy in copies[j + 1]:
                copy.wait()
        start = j * chunk
        count = chunk if j < 3 else chunk // 2
        carry = loop(count, lambda k, c: step(start + k, c), carry, count)
        if j == 3:
            for k in range(start + count, levels - 1):
                carry = step(k, carry)
            inflow, before, kept_p, kept_v = carry
            here = first + sign * (levels - 1)
            at = lax.rem(here, half_levels)
            kept_p = jnp.where(block == at, pltpu.roll(fields[here, 3], 4 * at, 1), kept_p)
            kept_v = jnp.where(block == at, pltpu.roll(fields[here, 1], 4 * at, 1), kept_v)
            weight = weights[here]
            inverse = 1.0 / (weight + inflow)
            part_a[here] = weight * inverse
            part_b[here] = before * inverse
            part_c[here] = inverse
            carry = (inflow, before, kept_p, kept_v)
        if j % 2:
            half = top + sign * (j // 2)
            rows = pl.multiple_of(16 * half, 16)
            edges[pl.ds(rows, 16), :] = carry[2]
            edges[pl.ds(32 + rows, 16), :] = carry[3]
            carry = (carry[0], carry[1], empty, empty)
    outward = jnp.where(top == 0, 1.0 / pair[levels - 1], zeros)
    resist[...] = inverse + outward

    own = jnp.where(block == 0, own_metric[...], 0.0)
    for shift in (4, 8, 16, 32, 64):
        own = own + pltpu.roll(own, shift, 1)
    edges[64:80, :] = own
    place = lax.rem(lane_ids(16) + 2, 4)
    for half in range(2):
        at = 16 * half
        p = edges[at : at + 16, :]
        v = edges[32 + at : 48 + at, :]
        sides[0, at : at + 16, :] = jnp.where(
            place < 2, p, jnp.where(place == 2, pltpu.roll(v, 1, 1), pltpu.roll(own, 2, 1))
        )
        sides[1, at : at + 16, :] = jnp.where(
            place >= 2, p, jnp.where(place == 1, pltpu.roll(v, 127, 1), pltpu.roll(own, 126, 1))
        )
    for copy in late:
        copy.wait()


def pack_y(sides, low_halo, high_halo, on_chip, off_chip, ends):
    levels = (low_halo.shape[0] - 8) // 3
    block = block_of(8)
    row = row_ids(8)
    kept = jnp.zeros((8, 128), f32)
    for half in range(2):

        def gather(i, kept):
            moved = []
            for j in range(32):
                at = 32 * i + j
                level = half * (levels // 2) + at
                low = jnp.broadcast_to(low_halo[pl.ds(2 * level + 1, 1), :], (8, 128))
                high = jnp.broadcast_to(high_halo[pl.ds(2 * level, 1), :], (8, 128))
                both = pltpu.roll(jnp.where(row == 2 * half, low, high), 4 * at, 1)
                moved.append(((block == at) & (row // 2 == half), both))
            for mine, both in moved:
                kept = jnp.where(mine, both, kept)
            return kept

        kept = lax.fori_loop(0, levels // 64, gather, kept)
    odd = lax.rem(lax.axis_index("gy"), 2)
    for out, side in ((on_chip, odd), (off_chip, 1 - odd)):
        out[0:32, :] = sides[side]
        out[32:40, :] = kept
    ends[...] = kept


def interior(fields, low_halo, high_halo, metric, part_a, part_b, done, reach):
    levels = fields.shape[0]
    top, sign, first, link = order(levels)
    row = row_ids(16)
    m = metric[...]
    slope = step_dt * 0.5 * m
    spread = 0.5 * step_dt * sound_sq * m * m
    spread_first, spread_last = spread[0:1], spread[15:16]
    spread_below, spread_above = pltpu.roll(spread, 1, 0), pltpu.roll(spread, 15, 0)
    spread_west, spread_east = pltpu.roll(spread, 1, 1), pltpu.roll(spread, 127, 1)
    slope_low = step_dt * 0.5 * low_halo[3 * levels : 3 * levels + 1, :]
    slope_high = step_dt * 0.5 * high_halo[3 * levels : 3 * levels + 1, :]
    batch = 16

    def east(z):
        return pltpu.roll(z, 127, 1)

    def west(z):
        return pltpu.roll(z, 1, 1)

    def below(z, edge):
        return jnp.where(row == 0, edge, pltpu.roll(z, 1, 0))

    def above(z, edge):
        return jnp.where(row == 15, edge, pltpu.roll(z, 15, 0))

    def several(i, d):
        ls = [first + sign * (i * batch + j) for j in range(batch)]
        pieces = []
        for l in ls:
            pieces.append(
                (
                    fields[l, 3],
                    fields[l, 0],
                    fields[l, 1],
                    low_halo[pl.ds(2 * l + 1, 1), :],
                    low_halo[pl.ds(2 * l, 1), :],
                    low_halo[pl.ds(2 * levels + l, 1), :],
                    high_halo[pl.ds(2 * l, 1), :],
                    high_halo[pl.ds(2 * l + 1, 1), :],
                    high_halo[pl.ds(2 * levels + l, 1), :],
                    [part_a[l, f] for f in range(4)],
                    [part_b[l, f] for f in range(4)],
                    fields[l, 2],
                )
            )
        results = []
        for p, u, v, near_low, far_low, u_low, near_high, far_high, u_high, a, b, w in pieces:
            before = below(p, near_low)
            after = above(p, near_high)
            sides = before + after
            p_east, p_west = east(p), west(p)
            u1 = u - slope * (after - before)
            v1 = v - slope * (p_east - p_west)
            u1_low = u_low - slope_low * (p[0:1] - far_low)
            u1_high = u_high - slope_high * (far_high - p[15:16])
            inner = hyper_nu * ((p_east + p_west) + 2.0 * sides - 8.0 * p)
            p1 = (
                (1.0 - 18.0 * hyper_nu) * p
                + 8.0 * hyper_nu * sides
                - above(u1 * spread_below + hyper_nu * after, u1_high * spread_last + hyper_nu * far_high)
                + below(u1 * spread_above - hyper_nu * before, u1_low * spread_first - hyper_nu * far_low)
                - east(v1 * spread_west + inner)
                + west(v1 * spread_east - inner)
            )
            results.append(([a[f] * z for f, z in enumerate((u1, v1, w, p1))], b))
        for l, (drive, b) in zip(ls, results):
            d = tuple(drive[f] + b[f] * d[f] for f in range(4))
            for f in range(4):
                done[l, f] = d[f]
        return d

    zeros = jnp.zeros((16, 128), f32)
    loop(levels // batch, several, (zeros,) * 4, 1)

    block = block_of(16)

    reach_batch = 32

    def segment(half, onward):
        def gather(i, carry):
            (on_v, on_p), (kept_v, kept_p) = carry
            moved = []
            for j in range(reach_batch):
                k = levels - 1 - ((1 - half) * (levels // 2) + i * reach_batch + j)
                l = first + sign * k
                at = lax.rem(l, levels // 2)
                moved.append(
                    (block == at, pltpu.roll(part_a[l, 1] * on_v, 4 * at, 1), pltpu.roll(part_a[l, 3] * on_p, 4 * at, 1))
                )
                on_v = part_b[l, 1] * on_v
                on_p = part_b[l, 3] * on_p
            for mine, v, p in moved:
                kept_v = jnp.where(mine, v, kept_v)
                kept_p = jnp.where(mine, p, kept_p)
            return (on_v, on_p), (kept_v, kept_p)

        onward, kept = lax.fori_loop(0, levels // (2 * reach_batch), gather, (onward, (zeros, zeros)))
        at = half + top * (1 - 2 * half)
        reach[0, at] = kept[0]
        reach[1, at] = kept[1]
        return onward

    ones = jnp.ones((16, 128), f32)
    segment(0, segment(1, (ones, ones)))


def finish_forward(done, edges, ends, off_chip, on_chip, reach, resist, out, fixes):
    levels = done.shape[0]
    top, sign, first, link = order(levels)
    turn = lax.axis_index("gy")
    odd = lax.rem(turn, 2) == 1
    near_side, far_side = on_chip[...], off_chip[...]
    left = jnp.where(turn == 0, 0.0, jnp.where(odd, near_side, far_side))
    right = jnp.where(turn == lax.axis_size("gy") - 1, 0.0, jnp.where(odd, far_side, near_side))
    lane = lane_ids(16)
    row = row_ids(16)
    place = lax.rem(lane + 2, 4)
    m = edges[64:80, :]
    slope = step_dt * 0.5 * m
    spread = 0.5 * step_dt * sound_sq * m * m

    def shift(z, by):
        return pltpu.roll(z, by % 128, 1)

    for half in range(2):
        at = 16 * half

        def sides_of(side):
            p = side[at : at + 16, :] - edges[at : at + 16, :]
            low = side[32 + 2 * half : 33 + 2 * half, :] - ends[2 * half : 2 * half + 1, :]
            high = side[33 + 2 * half : 34 + 2 * half, :] - ends[2 * half + 1 : 2 * half + 2, :]
            before = jnp.where(row == 0, low, pltpu.roll(p, 1, 0))
            after = jnp.where(row == 15, high, pltpu.roll(p, 15, 0))
            return p, 2.0 * (before + after) - 8.0 * p

        p_own = edges[at : at + 16, :]
        p_left, cross_left = sides_of(left)
        p_right, cross_right = sides_of(right)
        p_east, p_west = shift(p_own, -1), shift(p_own, 1)
        v1_own = edges[32 + at : 48 + at, :] - slope * (p_east - p_west)
        from_left, from_right = left[at : at + 16, :], right[at : at + 16, :]
        slope_left = step_dt * 0.5 * shift(from_left, -2)
        slope_right = step_dt * 0.5 * shift(from_right, 2)
        v1_left = shift(from_left, -1) - slope_left * (p_east - shift(from_left, 1))
        v1_right = shift(from_right, 1) - slope_right * (shift(from_right, -1) - p_west)
        second = (
            jnp.where(place >= 2, shift(p_left, 2), shift(p_right, -2))
            + jnp.where(place == 2, shift(cross_left, 1), 0.0)
            + jnp.where(place == 1, shift(cross_right, -1), 0.0)
        )
        own_v = jnp.where(
            place == 2, slope * shift(p_left, 1), jnp.where(place == 1, -slope * shift(p_right, -1), 0.0)
        )
        diff_v = jnp.where(
            place == 2,
            shift(v1_own - v1_left, 1),
            jnp.where(
                place == 3,
                -shift(own_v, 1),
                jnp.where(place == 1, shift(v1_right - v1_own, -1), shift(own_v, -1)),
            ),
        )
        fix_p = -spread * diff_v - hyper_nu * second
        fixes[0, half] = own_v
        fixes[1, half] = fix_p
        sum_v = reach[0, half] * own_v + (sum_v if half else 0.0)
        sum_p = reach[1, half] * fix_p + (sum_p if half else 0.0)

    for steps in ((4, 8, 12, 16, 20, 24, 28), (32, 64, 96)):
        sum_v = sum([shift(sum_v, by) for by in steps], sum_v)
        sum_p = sum([shift(sum_p, by) for by in steps], sum_p)
    edge = (lane >= 126) | (lane < 2)
    last = done[first + sign * (levels - 1)]
    out[0, 0] = last[0]
    out[0, 1] = last[1] + jnp.where(edge, sum_v, 0.0)
    out[0, 2] = last[2]
    out[0, 3] = last[3] + jnp.where(edge, sum_p, 0.0)
    out[1] = resist[...]


def settle(before, part_a, part_b, fixes, done):
    levels = before.shape[0]
    top, sign, first, link = order(levels)
    lane = lane_ids(16)
    edge = (lane >= 126) | (lane < 2)
    batch = 16

    def segment(turn, carry):
        half = top + sign * turn
        all_v = fixes[0, half]
        all_p = fixes[1, half]

        def several(i, carry):
            e_v, e_p = carry
            ls = [first + sign * (turn * (levels // 2) + i * batch + j) for j in range(batch)]
            drives = []
            for l in ls:
                back = lax.rem(128 - 4 * (l - half * (levels // 2)), 128)
                v1 = jnp.where(edge, pltpu.roll(all_v, back, 1), 0.0)
                p1 = jnp.where(edge, pltpu.roll(all_p, back, 1), 0.0)
                drives.append(
                    (part_a[l, 1] * v1, part_b[l, 1], part_a[l, 3] * p1, part_b[l, 3], before[l, 1], before[l, 3])
                )
            for l, (drive_v, b_v, drive_p, b_p, d_v, d_p) in zip(ls, drives):
                e_v = drive_v + b_v * e_v
                e_p = drive_p + b_p * e_p
                done[l, 1] = d_v + e_v
                done[l, 3] = d_p + e_p
            return e_v, e_p

        return lax.fori_loop(0, levels // (2 * batch), several, carry)

    zeros = jnp.zeros((16, 128), f32)
    segment(1, segment(0, (zeros, zeros)))


def back_substitute(done, part_c, mine, other, out, x_ref, sems):
    levels = done.shape[0]
    top, sign, first, link = order(levels)
    last = first + sign * (levels - 1)
    x = mine[0] + (other[0] - mine[0]) * (part_c[last] / (mine[1] + other[1]))
    x_ref[last] = x
    chunk = levels // 8
    copies = []

    def several(ks, x):
        ls = [last - sign * k for k in ks]
        loaded = [(part_c[l], done[l]) for l in ls]
        for l, (c, d) in zip(ls, loaded):
            x = d + c * x
            x_ref[l] = x
        return x

    for j in range(8):
        ks = list(range(j * chunk + (j == 0), (j + 1) * chunk))
        for i in range(0, len(ks), 4):
            x = several(ks[i : i + 4], x)
        at = pl.ds((1 - top) * (levels - chunk) - sign * (j * chunk), chunk)
        copy = pltpu.make_async_copy(x_ref.at[at], out.at[at], sems.at[j])
        copy.start()
        copies.append(copy)
    for copy in copies:
        copy.wait()


def near(shape):
    return pltpu.VMEM(shape, f32)


def plain(shape):
    return jax.ShapeDtypeStruct(shape, f32)


def call(body, ins, outs, scratch=(), cost=0, name=None, aliases=None):
    def run(*args):
        return pl.pallas_call(
            body,
            in_specs=ins,
            out_specs=[VM] * len(outs),
            out_shape=outs,
            scratch_shapes=list(scratch),
            name=name,
            input_output_aliases=aliases or {},
            cost_estimate=pl.CostEstimate(flops=cost, bytes_accessed=cost, transcendentals=0) if cost else None,
            compiler_params=pltpu.CompilerParams(vmem_limit_bytes=LIMIT),
        )(*args)

    return run


def far(x):
    return pltpu.with_memory_space_constraint(x, pltpu.HBM)


def shards(state, metric, couple, base):
    levels = state.shape[0]
    nx, ny = lax.axis_size("gx"), lax.axis_size("gy")
    dma = pltpu.SemaphoreType.DMA
    side = (3 * levels + 8, 128)
    full = (levels, 4, 16, 128)
    state, metric, couple, base = far(state), far(metric), far(couple), far(base)

    low_side, high_side = call(
        pack_x, [HB, HB], [plain(side), plain(side)], [dma((6,))], name="pack_x"
    )(state, metric)
    low_halo = lax.ppermute(high_side, "gx", [(i, (i + 1) % nx) for i in range(nx)])
    high_halo = lax.ppermute(low_side, "gx", [((i + 1) % nx, i) for i in range(nx)])

    fields, own_metric, part_a, part_b, part_c, edges, sides, resist = call(
        factor,
        [HB, HB, HB, HB],
        [near(full), near((16, 128)), near(full), near(full), near(full), near((80, 128)), near((2, 32, 128)), near((4, 16, 128))],
        [pltpu.VMEM(full, f32), pltpu.VMEM(full, f32), dma((13,))],
        cost=8 * 1024 * 1024,
        name="factor",
    )(state, couple, base, metric)

    part = (40, 128)
    on_chip, off_chip, ends = call(
        pack_y, [VM] * 3, [plain(part), plain(part), near((8, 128))], name="pack_y"
    )(sides, low_halo, high_halo)
    swaps = []
    for i in range(nx):
        for j in range(ny):
            there = (i ^ 1, j) if j in (0, ny - 1) else (i, j + 1 if j % 2 else j - 1)
            swaps.append((i * ny + j, there[0] * ny + there[1]))
    off_chip = lax.ppermute(off_chip, ("gx", "gy"), swaps)
    on_chip = lax.ppermute(on_chip, "gy", [(j, j ^ 1) for j in range(ny)])

    edge = (2, 2, 16, 128)
    done, reach = call(
        interior,
        [VM] * 6,
        [near(full), near(edge)],
        cost=8 * 1024 * 1024,
        name="interior",
    )(fields, low_halo, high_halo, own_metric, part_a, part_b)

    mine, fixes = call(
        finish_forward,
        [VM] * 7,
        [plain((2, 4, 16, 128)), near(edge)],
        name="finish_forward",
    )(done, edges, ends, off_chip, on_chip, reach, resist)
    other = lax.ppermute(mine, "gz", [(0, 1), (1, 0)])

    done = call(
        settle,
        [VM] * 4,
        [near(full)],
        cost=8 * 1024 * 1024,
        name="settle",
        aliases={0: 0},
    )(done, part_a, part_b, fixes)[0]

    return pl.pallas_call(
        back_substitute,
        in_specs=[VM] * 4,
        out_specs=pl.BlockSpec(memory_space=pl.ANY),
        out_shape=plain(full),
        scratch_shapes=[pltpu.VMEM(full, f32), dma((8,))],
        name="back_substitute",
        compiler_params=pltpu.CompilerParams(vmem_limit_bytes=LIMIT),
    )(done, part_c, mine, other)


def solution(mesh):
    in_specs = (
        P("gz", None, "gx", "gy"),
        P("gx", "gy"),
        P("gz", None, "gx", "gy"),
        P("gz", None, "gx", "gy"),
    )
    out_specs = P("gz", None, "gx", "gy")
    return jax.shard_map(shards, mesh=mesh, in_specs=in_specs, out_specs=out_specs, check_vma=False)
```

```python
import functools

import jax
import jax.numpy as jnp
from jax import lax
from jax.experimental import pallas as pl
from jax.experimental.pallas import tpu as pltpu
from jax.sharding import PartitionSpec as P

step_dt = 0.5
sound_sq = 1.0
hyper_nu = 0.01

f32 = jnp.float32
HB = pl.BlockSpec(memory_space=pltpu.HBM)
VM = pl.BlockSpec(memory_space=pltpu.VMEM)
LIMIT = 32 * 1024 * 1024


def loop(count, body, carry, unroll):
    assert count % unroll == 0

    def several(i, carry):
        for j in range(unroll):
            carry = body(i * unroll + j, carry)
        return carry

    return lax.fori_loop(0, count // unroll, several, carry)


def row_ids(rows):
    return lax.broadcasted_iota(jnp.int32, (rows, 128), 0)


def lane_ids(rows):
    return lax.broadcasted_iota(jnp.int32, (rows, 128), 1)


def order(levels):
    top = lax.axis_index("gz")
    sign = 1 - 2 * top
    return top, sign, top * (levels - 1), top * (levels - 2)


def pack_x(state, metric, low_side, high_side, sems):
    levels = state.shape[0]
    copies = []
    for out, rows in ((low_side, (0, 1, 0)), (high_side, (15, 14, 15))):
        for part, (field, row) in enumerate(zip((3, 3, 0), rows)):
            copies.append((state.at[:, field, row], out.at[pl.ds(part * levels, levels)]))
        copies.append((metric.at[pl.ds(rows[0], 1)], out.at[pl.ds(3 * levels, 1)]))
    copies = [pltpu.make_async_copy(src, dst, sems.at[i]) for i, (src, dst) in enumerate(copies)]
    for copy in copies:
        copy.start()
    for copy in copies:
        copy.wait()


def block_of(rows):
    return lax.rem(lane_ids(rows) + 2, 128) // 4


def factor(state, couple, base, metric, fields, own_metric, part_a, part_b, part_c, edges, sides, resist, pair, weights, sems):
    levels = fields.shape[0]
    top, sign, first, link = order(levels)
    chunk = levels // 4
    early = [
        pltpu.make_async_copy(state.at[:, field], fields.at[:, field], sems.at[8 + i]) for i, field in enumerate((3, 1))
    ]
    early.append(pltpu.make_async_copy(metric, own_metric, sems.at[10]))
    late = [
        pltpu.make_async_copy(state.at[:, field], fields.at[:, field], sems.at[11 + i]) for i, field in enumerate((0, 2))
    ]
    copies = []
    for j in range(4):
        at = pl.ds(top * (levels - chunk) + sign * (j * chunk), chunk)
        copies.append(
            [
                pltpu.make_async_copy(couple.at[at], pair.at[at], sems.at[2 * j]),
                pltpu.make_async_copy(base.at[at], weights.at[at], sems.at[2 * j + 1]),
            ]
        )
    for copy in early + [copy for group in copies for copy in group] + late:
        copy.start()

    block = block_of(16)
    half_levels = levels // 2

    def step(k, carry):
        inflow, before, kept_p, kept_v = carry
        here = first + sign * k
        weight = weights[here]
        after = pair[link + sign * k]
        p, v = fields[here, 3], fields[here, 1]
        inverse = 1.0 / ((weight + after) + inflow)
        pushed = after * (weight + inflow)
        at = lax.rem(here, half_levels)
        mine = block == at
        kept_p = jnp.where(mine, pltpu.roll(p, 4 * at, 1), kept_p)
        kept_v = jnp.where(mine, pltpu.roll(v, 4 * at, 1), kept_v)
        part_a[here] = weight * inverse
        part_b[here] = before * inverse
        part_c[here] = after * inverse
        return pushed * inverse, after, kept_p, kept_v

    for copy in early:
        copy.wait()
    zeros = jnp.zeros((4, 16, 128), f32)
    empty = jnp.zeros((16, 128), f32)
    carry = (zeros, zeros, empty, empty)
    for j in range(4):
        if j == 0:
            for copy in copies[0] + copies[1]:
                copy.wait()
        elif j < 3:
            for copy in copies[j + 1]:
                copy.wait()
        start = j * chunk
        count = chunk if j < 3 else chunk // 2
        carry = loop(count, lambda k, c: step(start + k, c), carry, count)
        if j == 3:
            for k in range(start + count, levels - 1):
                carry = step(k, carry)
            inflow, before, kept_p, kept_v = carry
            here = first + sign * (levels - 1)
            at = lax.rem(here, half_levels)
            kept_p = jnp.where(block == at, pltpu.roll(fields[here, 3], 4 * at, 1), kept_p)
            kept_v = jnp.where(block == at, pltpu.roll(fields[here, 1], 4 * at, 1), kept_v)
            weight = weights[here]
            inverse = 1.0 / (weight + inflow)
            part_a[here] = weight * inverse
            part_b[here] = before * inverse
            part_c[here] = inverse
            carry = (inflow, before, kept_p, kept_v)
        if j % 2:
            half = top + sign * (j // 2)
            rows = pl.multiple_of(16 * half, 16)
            edges[pl.ds(rows, 16), :] = carry[2]
            edges[pl.ds(32 + rows, 16), :] = carry[3]
            carry = (carry[0], carry[1], empty, empty)
    outward = jnp.where(top == 0, 1.0 / pair[levels - 1], zeros)
    resist[...] = inverse + outward

    own = jnp.where(block == 0, own_metric[...], 0.0)
    for shift in (4, 8, 16, 32, 64):
        own = own + pltpu.roll(own, shift, 1)
    edges[64:80, :] = own
    place = lax.rem(lane_ids(16) + 2, 4)
    for half in range(2):
        at = 16 * half
        p = edges[at : at + 16, :]
        v = edges[32 + at : 48 + at, :]
        sides[0, at : at + 16, :] = jnp.where(
            place < 2, p, jnp.where(place == 2, pltpu.roll(v, 1, 1), pltpu.roll(own, 2, 1))
        )
        sides[1, at : at + 16, :] = jnp.where(
            place >= 2, p, jnp.where(place == 1, pltpu.roll(v, 127, 1), pltpu.roll(own, 126, 1))
        )
    for copy in late:
        copy.wait()


def pack_y(sides, low_halo, high_halo, on_chip, off_chip, ends):
    levels = (low_halo.shape[0] - 8) // 3
    block = block_of(8)
    row = row_ids(8)
    kept = jnp.zeros((8, 128), f32)
    for half in range(2):

        def gather(i, kept):
            moved = []
            for j in range(32):
                at = 32 * i + j
                level = half * (levels // 2) + at
                low = jnp.broadcast_to(low_halo[pl.ds(level, 1), :], (8, 128))
                high = jnp.broadcast_to(high_halo[pl.ds(level, 1), :], (8, 128))
                both = pltpu.roll(jnp.where(row == 2 * half, low, high), 4 * at, 1)
                moved.append(((block == at) & (row // 2 == half), both))
            for mine, both in moved:
                kept = jnp.where(mine, both, kept)
            return kept

        kept = lax.fori_loop(0, levels // 64, gather, kept)
    odd = lax.rem(lax.axis_index("gy"), 2)
    for out, side in ((on_chip, odd), (off_chip, 1 - odd)):
        out[0:32, :] = sides[side]
        out[32:40, :] = kept
    ends[...] = kept


def interior(fields, low_halo, high_halo, metric, part_a, part_b, done, reach):
    levels = fields.shape[0]
    top, sign, first, link = order(levels)
    row = row_ids(16)
    m = metric[...]
    slope = step_dt * 0.5 * m
    spread = 0.5 * step_dt * sound_sq * m * m
    spread_first, spread_last = spread[0:1], spread[15:16]
    spread_below, spread_above = pltpu.roll(spread, 1, 0), pltpu.roll(spread, 15, 0)
    spread_west, spread_east = pltpu.roll(spread, 1, 1), pltpu.roll(spread, 127, 1)
    slope_low = step_dt * 0.5 * low_halo[3 * levels : 3 * levels + 1, :]
    slope_high = step_dt * 0.5 * high_halo[3 * levels : 3 * levels + 1, :]
    batch = 16

    def east(z):
        return pltpu.roll(z, 127, 1)

    def west(z):
        return pltpu.roll(z, 1, 1)

    def below(z, edge):
        return jnp.where(row == 0, edge, pltpu.roll(z, 1, 0))

    def above(z, edge):
        return jnp.where(row == 15, edge, pltpu.roll(z, 15, 0))

    def several(i, d):
        ls = [first + sign * (i * batch + j) for j in range(batch)]
        pieces = []
        for l in ls:
            pieces.append(
                (
                    fields[l, 3],
                    fields[l, 0],
                    fields[l, 1],
                    low_halo[pl.ds(l, 1), :],
                    low_halo[pl.ds(levels + l, 1), :],
                    low_halo[pl.ds(2 * levels + l, 1), :],
                    high_halo[pl.ds(l, 1), :],
                    high_halo[pl.ds(levels + l, 1), :],
                    high_halo[pl.ds(2 * levels + l, 1), :],
                    [part_a[l, f] for f in range(4)],
                    [part_b[l, f] for f in range(4)],
                    fields[l, 2],
                )
            )
        results = []
        for p, u, v, near_low, far_low, u_low, near_high, far_high, u_high, a, b, w in pieces:
            before = below(p, near_low)
            after = above(p, near_high)
            sides = before + after
            p_east, p_west = east(p), west(p)
            u1 = u - slope * (after - before)
            v1 = v - slope * (p_east - p_west)
            u1_low = u_low - slope_low * (p[0:1] - far_low)
            u1_high = u_high - slope_high * (far_high - p[15:16])
            inner = hyper_nu * ((p_east + p_west) + 2.0 * sides - 8.0 * p)
            p1 = (
                (1.0 - 18.0 * hyper_nu) * p
                + 8.0 * hyper_nu * sides
                - above(u1 * spread_below + hyper_nu * after, u1_high * spread_last + hyper_nu * far_high)
                + below(u1 * spread_above - hyper_nu * before, u1_low * spread_first - hyper_nu * far_low)
                - east(v1 * spread_west + inner)
                + west(v1 * spread_east - inner)
            )
            results.append(([a[f] * z for f, z in enumerate((u1, v1, w, p1))], b))
        for l, (drive, b) in zip(ls, results):
            d = tuple(drive[f] + b[f] * d[f] for f in range(4))
            for f in range(4):
                done[l, f] = d[f]
        return d

    zeros = jnp.zeros((16, 128), f32)
    loop(levels // batch, several, (zeros,) * 4, 1)

    block = block_of(16)

    reach_batch = 32

    def segment(half, onward):
        def gather(i, carry):
            (on_v, on_p), (kept_v, kept_p) = carry
            moved = []
            for j in range(reach_batch):
                k = levels - 1 - ((1 - half) * (levels // 2) + i * reach_batch + j)
                l = first + sign * k
                at = lax.rem(l, levels // 2)
                moved.append(
                    (block == at, pltpu.roll(part_a[l, 1] * on_v, 4 * at, 1), pltpu.roll(part_a[l, 3] * on_p, 4 * at, 1))
                )
                on_v = part_b[l, 1] * on_v
                on_p = part_b[l, 3] * on_p
            for mine, v, p in moved:
                kept_v = jnp.where(mine, v, kept_v)
                kept_p = jnp.where(mine, p, kept_p)
            return (on_v, on_p), (kept_v, kept_p)

        onward, kept = lax.fori_loop(0, levels // (2 * reach_batch), gather, (onward, (zeros, zeros)))
        at = half + top * (1 - 2 * half)
        reach[0, at] = kept[0]
        reach[1, at] = kept[1]
        return onward

    ones = jnp.ones((16, 128), f32)
    segment(0, segment(1, (ones, ones)))


def finish_forward(done, edges, ends, off_chip, on_chip, reach, resist, out, fixes):
    levels = done.shape[0]
    top, sign, first, link = order(levels)
    turn = lax.axis_index("gy")
    odd = lax.rem(turn, 2) == 1
    near_side, far_side = on_chip[...], off_chip[...]
    left = jnp.where(turn == 0, 0.0, jnp.where(odd, near_side, far_side))
    right = jnp.where(turn == lax.axis_size("gy") - 1, 0.0, jnp.where(odd, far_side, near_side))
    lane = lane_ids(16)
    row = row_ids(16)
    place = lax.rem(lane + 2, 4)
    m = edges[64:80, :]
    slope = step_dt * 0.5 * m
    spread = 0.5 * step_dt * sound_sq * m * m

    def shift(z, by):
        return pltpu.roll(z, by % 128, 1)

    for half in range(2):
        at = 16 * half

        def sides_of(side):
            p = side[at : at + 16, :] - edges[at : at + 16, :]
            low = side[32 + 2 * half : 33 + 2 * half, :] - ends[2 * half : 2 * half + 1, :]
            high = side[33 + 2 * half : 34 + 2 * half, :] - ends[2 * half + 1 : 2 * half + 2, :]
            before = jnp.where(row == 0, low, pltpu.roll(p, 1, 0))
            after = jnp.where(row == 15, high, pltpu.roll(p, 15, 0))
            return p, 2.0 * (before + after) - 8.0 * p

        p_own = edges[at : at + 16, :]
        p_left, cross_left = sides_of(left)
        p_right, cross_right = sides_of(right)
        p_east, p_west = shift(p_own, -1), shift(p_own, 1)
        v1_own = edges[32 + at : 48 + at, :] - slope * (p_east - p_west)
        from_left, from_right = left[at : at + 16, :], right[at : at + 16, :]
        slope_left = step_dt * 0.5 * shift(from_left, -2)
        slope_right = step_dt * 0.5 * shift(from_right, 2)
        v1_left = shift(from_left, -1) - slope_left * (p_east - shift(from_left, 1))
        v1_right = shift(from_right, 1) - slope_right * (shift(from_right, -1) - p_west)
        second = (
            jnp.where(place >= 2, shift(p_left, 2), shift(p_right, -2))
            + jnp.where(place == 2, shift(cross_left, 1), 0.0)
            + jnp.where(place == 1, shift(cross_right, -1), 0.0)
        )
        own_v = jnp.where(
            place == 2, slope * shift(p_left, 1), jnp.where(place == 1, -slope * shift(p_right, -1), 0.0)
        )
        diff_v = jnp.where(
            place == 2,
            shift(v1_own - v1_left, 1),
            jnp.where(
                place == 3,
                -shift(own_v, 1),
                jnp.where(place == 1, shift(v1_right - v1_own, -1), shift(own_v, -1)),
            ),
        )
        fix_p = -spread * diff_v - hyper_nu * second
        fixes[0, half] = own_v
        fixes[1, half] = fix_p
        sum_v = reach[0, half] * own_v + (sum_v if half else 0.0)
        sum_p = reach[1, half] * fix_p + (sum_p if half else 0.0)

    for steps in ((4, 8, 12, 16, 20, 24, 28), (32, 64, 96)):
        sum_v = sum([shift(sum_v, by) for by in steps], sum_v)
        sum_p = sum([shift(sum_p, by) for by in steps], sum_p)
    edge = (lane >= 126) | (lane < 2)
    last = done[first + sign * (levels - 1)]
    out[0, 0] = last[0]
    out[0, 1] = last[1] + jnp.where(edge, sum_v, 0.0)
    out[0, 2] = last[2]
    out[0, 3] = last[3] + jnp.where(edge, sum_p, 0.0)
    out[1] = resist[...]


def settle(before, part_a, part_b, fixes, done):
    levels = before.shape[0]
    top, sign, first, link = order(levels)
    lane = lane_ids(16)
    edge = (lane >= 126) | (lane < 2)
    batch = 16

    def segment(turn, carry):
        half = top + sign * turn
        all_v = fixes[0, half]
        all_p = fixes[1, half]

        def several(i, carry):
            e_v, e_p = carry
            ls = [first + sign * (turn * (levels // 2) + i * batch + j) for j in range(batch)]
            drives = []
            for l in ls:
                back = lax.rem(128 - 4 * (l - half * (levels // 2)), 128)
                v1 = jnp.where(edge, pltpu.roll(all_v, back, 1), 0.0)
                p1 = jnp.where(edge, pltpu.roll(all_p, back, 1), 0.0)
                drives.append(
                    (part_a[l, 1] * v1, part_b[l, 1], part_a[l, 3] * p1, part_b[l, 3], before[l, 1], before[l, 3])
                )
            for l, (drive_v, b_v, drive_p, b_p, d_v, d_p) in zip(ls, drives):
                e_v = drive_v + b_v * e_v
                e_p = drive_p + b_p * e_p
                done[l, 1] = d_v + e_v
                done[l, 3] = d_p + e_p
            return e_v, e_p

        return lax.fori_loop(0, levels // (2 * batch), several, carry)

    zeros = jnp.zeros((16, 128), f32)
    segment(1, segment(0, (zeros, zeros)))


def back_substitute(done, part_c, mine, other, out, x_ref, sems):
    levels = done.shape[0]
    top, sign, first, link = order(levels)
    last = first + sign * (levels - 1)
    x = mine[0] + (other[0] - mine[0]) * (part_c[last] / (mine[1] + other[1]))
    x_ref[last] = x
    chunk = levels // 8
    copies = []

    def several(ks, x):
        ls = [last - sign * k for k in ks]
        loaded = [(part_c[l], done[l]) for l in ls]
        for l, (c, d) in zip(ls, loaded):
            x = d + c * x
            x_ref[l] = x
        return x

    for j in range(8):
        ks = list(range(j * chunk + (j == 0), (j + 1) * chunk))
        for i in range(0, len(ks), 8):
            x = several(ks[i : i + 8], x)
        at = pl.ds((1 - top) * (levels - chunk) - sign * (j * chunk), chunk)
        copy = pltpu.make_async_copy(x_ref.at[at], out.at[at], sems.at[j])
        copy.start()
        copies.append(copy)
    for copy in copies:
        copy.wait()


def near(shape):
    return pltpu.VMEM(shape, f32)


def plain(shape):
    return jax.ShapeDtypeStruct(shape, f32)


def call(body, ins, outs, scratch=(), cost=0, name=None, aliases=None):
    def run(*args):
        return pl.pallas_call(
            body,
            in_specs=ins,
            out_specs=[VM] * len(outs),
            out_shape=outs,
            scratch_shapes=list(scratch),
            name=name,
            input_output_aliases=aliases or {},
            cost_estimate=pl.CostEstimate(flops=cost, bytes_accessed=cost, transcendentals=0) if cost else None,
            compiler_params=pltpu.CompilerParams(vmem_limit_bytes=LIMIT),
        )(*args)

    return run


def far(x):
    return pltpu.with_memory_space_constraint(x, pltpu.HBM)


def shards(state, metric, couple, base):
    levels = state.shape[0]
    nx, ny = lax.axis_size("gx"), lax.axis_size("gy")
    dma = pltpu.SemaphoreType.DMA
    side = (3 * levels + 8, 128)
    full = (levels, 4, 16, 128)
    state, metric, couple, base = far(state), far(metric), far(couple), far(base)

    low_side, high_side = call(
        pack_x, [HB, HB], [plain(side), plain(side)], [dma((8,))], name="pack_x"
    )(state, metric)
    low_halo = lax.ppermute(high_side, "gx", [(i, (i + 1) % nx) for i in range(nx)])
    high_halo = lax.ppermute(low_side, "gx", [((i + 1) % nx, i) for i in range(nx)])

    fields, own_metric, part_a, part_b, part_c, edges, sides, resist = call(
        factor,
        [HB, HB, HB, HB],
        [near(full), near((16, 128)), near(full), near(full), near(full), near((80, 128)), near((2, 32, 128)), near((4, 16, 128))],
        [pltpu.VMEM(full, f32), pltpu.VMEM(full, f32), dma((13,))],
        cost=8 * 1024 * 1024,
        name="factor",
    )(state, couple, base, metric)

    part = (40, 128)
    on_chip, off_chip, ends = call(
        pack_y, [VM] * 3, [plain(part), plain(part), near((8, 128))], name="pack_y"
    )(sides, low_halo, high_halo)
    swaps = []
    for i in range(nx):
        for j in range(ny):
            there = (i ^ 1, j) if j in (0, ny - 1) else (i, j + 1 if j % 2 else j - 1)
            swaps.append((i * ny + j, there[0] * ny + there[1]))
    off_chip = lax.ppermute(off_chip, ("gx", "gy"), swaps)
    on_chip = lax.ppermute(on_chip, "gy", [(j, j ^ 1) for j in range(ny)])

    edge = (2, 2, 16, 128)
    done, reach = call(
        interior,
        [VM] * 6,
        [near(full), near(edge)],
        cost=8 * 1024 * 1024,
        name="interior",
    )(fields, low_halo, high_halo, own_metric, part_a, part_b)

    mine, fixes = call(
        finish_forward,
        [VM] * 7,
        [plain((2, 4, 16, 128)), near(edge)],
        name="finish_forward",
    )(done, edges, ends, off_chip, on_chip, reach, resist)
    other = lax.ppermute(mine, "gz", [(0, 1), (1, 0)])

    done = call(
        settle,
        [VM] * 4,
        [near(full)],
        cost=8 * 1024 * 1024,
        name="settle",
        aliases={0: 0},
    )(done, part_a, part_b, fixes)[0]

    return pl.pallas_call(
        back_substitute,
        in_specs=[VM] * 4,
        out_specs=pl.BlockSpec(memory_space=pl.ANY),
        out_shape=plain(full),
        scratch_shapes=[pltpu.VMEM(full, f32), dma((8,))],
        name="back_substitute",
        compiler_params=pltpu.CompilerParams(vmem_limit_bytes=LIMIT),
    )(done, part_c, mine, other)


def solution(mesh):
    in_specs = (
        P("gz", None, "gx", "gy"),
        P("gx", "gy"),
        P("gz", None, "gx", "gy"),
        P("gz", None, "gx", "gy"),
    )
    out_specs = P("gz", None, "gx", "gy")
    return jax.shard_map(shards, mesh=mesh, in_specs=in_specs, out_specs=out_specs, check_vma=False)
```
